256 devices in a mesh: img: 4 (over x), gs: 64 (over y, z, core).
Axes of the slice: x: 4, y: 4, z: 8, core: 2. Of those that a mesh axis runs over, the one named last changes fastest.
Arguments:
- params: float32 [59, 262144], P(None, 'gs'), may hold values from -4 to 1
- adam_m: float32 [59, 262144], P(None, 'gs'), may hold values from -3 to 3
- adam_v: float32 [59, 262144], P(None, 'gs'), may hold values from 0.01 to 1
- cameras: float32 [16, 16], replicated, may hold values from -4.5 to 307.2
- device_camera: int32 [4, 64], P('img'), may hold values from 0 to 15
- send_index: int32 [4, 64, 64, 64], P('img', 'gs'), may hold values from 0 to 4095
- slot_rows: int32 [4, 64, 32, 256], P('img', 'gs'), may hold values from -1 to 4095, as said below
- tile_ids: int32 [4, 64, 32], P('img', 'gs'), may hold values from 0 to 255
- target: float32 [4, 64, 32, 3, 256], P('img', 'gs'), may hold values from 0 to 1
Outputs:
- new_params: float32 [59, 262144], P(None, 'gs')
- new_m: float32 [59, 262144], P(None, 'gs')
- new_v: float32 [59, 262144], P(None, 'gs')
- rendered: float32 [4, 64, 32, 3, 256], P('img', 'gs')
The draws below stay inside these ranges and needn't reach their ends.
Inputs may be any that keep to these rules, and one draw needn't show every extreme that they name: `slot_rows`: in each tile the live slots come first; every tile has a live slot, and the first tile of every device has all 256 live.
All inputs are finite; a program needn't handle non-finite values.
Results may differ from the reference program's by a relative error of at most 0.0003.
Values sent between devices are 32-bit elements; how exact they have to be, the bound alone decides.
No kernel may reach another device: no remote copies, remote signals or barrier semaphores. Data moves between devices by JAX's collectives and lax.ppermute only.
A program may use at most 64 MiB of HBM per device.

```python
import math
import jax
import jax.numpy as jnp
import numpy as np
from jax import lax

PARAMS = 59
TILE = 16
IMG_TILES = 16
N_CAM = 16
SLOTS = 256
G_DEV = 4096
TILE_DEV = 32
CAP = 64
ROWS = 4096
GAUSS = 262144
N_IMG = 4
N_GS = 64


def draw_params(key, part):
    key = jax.random.fold_in(key, 11)
    subkeys = jax.random.split(key, 5)
    position = jax.random.uniform(subkeys[0], (3, GAUSS), jnp.float32, -1.0, 1.0)
    log_scale = jax.random.uniform(subkeys[1], (3, GAUSS), jnp.float32, math.log(0.3), math.log(1.2))
    quaternion = jax.random.uniform(subkeys[2], (4, GAUSS), jnp.float32, -1.0, 1.0)
    opacity = jax.random.uniform(subkeys[3], (1, GAUSS), jnp.float32, -4.0, 0.0)
    colour = jnp.clip(0.3 * jax.random.normal(subkeys[4], (48, GAUSS), jnp.float32), -1.0, 1.0)
    return jnp.concatenate([position, log_scale, quaternion, opacity, colour], axis=0)


def draw_cameras(key, part):
    key = jax.random.fold_in(key, 12)
    subkeys = jax.random.split(key, 6)
    turn = jax.random.uniform(subkeys[0], (9, N_CAM), jnp.float32, -0.1, 0.1) + jnp.asarray(np.eye(3).reshape(9, 1), jnp.float32)
    shift_side = jax.random.uniform(subkeys[1], (2, N_CAM), jnp.float32, -0.3, 0.3)
    shift_depth = jax.random.uniform(subkeys[2], (1, N_CAM), jnp.float32, 3.5, 4.5)
    centre_side = jax.random.uniform(subkeys[3], (2, N_CAM), jnp.float32, -0.3, 0.3)
    centre_depth = jax.random.uniform(subkeys[4], (1, N_CAM), jnp.float32, -4.5, -3.5)
    focal = jax.random.uniform(subkeys[5], (1, N_CAM), jnp.float32, 0.8, 1.2) * (IMG_TILES * TILE)
    return jnp.concatenate([turn, shift_side, shift_depth, centre_side, centre_depth, focal], axis=0)


def draw_slot_rows(key, part):
    key = jax.random.fold_in(key, 13)
    subkeys = jax.random.split(key, 3)
    shape = (N_IMG, N_GS, TILE_DEV, SLOTS)
    longest = jax.random.randint(subkeys[0], (N_IMG, N_GS, 1), SLOTS // 4, SLOTS + 1)
    length = jax.random.randint(subkeys[1], (N_IMG, N_GS, TILE_DEV), 1, longest + 1)
    length = length.at[:, :, 0].set(SLOTS).at[:, :, 1].set(max(SLOTS // 4, 1))
    chosen = jax.random.randint(subkeys[2], shape, 0, ROWS)
    chosen = chosen.at[:, :, 0, 0].set(ROWS - 1)
    position = lax.broadcasted_iota(jnp.int32, shape, 3)
    return jnp.where(position < length[..., None], chosen, -1).astype(jnp.int32)


def touch_ends(drawn, stream_key, smallest, largest):
    longest = drawn.shape.index(max(drawn.shape))
    spots = []
    for shift in (0, 1):
        where = [jax.random.randint(jax.random.fold_in(stream_key, axis), (), 0, length) for axis, length in enumerate(drawn.shape)]
        where[longest] = (where[longest] + shift) % drawn.shape[longest]
        spots.append(tuple(where))
    return drawn.at[spots[0]].set(smallest).at[spots[1]].set(largest)


def steps_of(stream_key, dims, cuts, smallest, top_value):
    loudness = 1.0
    for dim, blocks in cuts:
        draws = jax.random.uniform(jax.random.fold_in(jax.random.fold_in(stream_key, 6), dim), (blocks,), jnp.float32, smallest / len(cuts), top_value / len(cuts))
        loudness = loudness * jnp.repeat(jnp.exp(draws), dims[dim] // blocks).reshape((-1,) + (1,) * (len(dims) - 1 - dim))
    return loudness


def scatter_about(key, shape, scale, reach, shards=(), held_as=jnp.bfloat16):
    drawn = scale * jax.random.normal(key, shape, jnp.float32)
    if shards:
        drawn = drawn * steps_of(key, shape, shards, -0.22, 0.18)
    return jnp.clip(drawn, -reach, reach).astype(held_as)


def setup_inputs(seed: int = 0) -> dict:
    arg_keys = jax.random.split(jax.random.key(seed), 10)
    return {
        "params": draw_params(jax.random.fold_in(arg_keys[9], 71), 0),
        "adam_m": scatter_about(arg_keys[1], (PARAMS, GAUSS), 0.5, 3.0, ((1, 64),), jnp.float32),
        "adam_v": jnp.clip(jnp.exp(math.log(1.0) - 4.6051702 * jax.random.uniform(arg_keys[2], (PARAMS, GAUSS), jnp.float32) ** steps_of(arg_keys[2], (PARAMS, GAUSS), ((1, 64),), -0.2, 0.2)), 0.01, 1.0),
        "cameras": draw_cameras(jax.random.fold_in(arg_keys[9], 71), 0),
        "device_camera": touch_ends(jax.random.randint(arg_keys[4], (N_IMG, N_GS), 0, N_CAM), jax.random.fold_in(arg_keys[4], 1), 0, N_CAM - 1).astype(jnp.int32),
        "send_index": touch_ends(jax.random.randint(arg_keys[5], (N_IMG, N_GS, N_GS, CAP), 0, G_DEV), jax.random.fold_in(arg_keys[5], 1), 0, G_DEV - 1).astype(jnp.int32),
        "slot_rows": draw_slot_rows(jax.random.fold_in(arg_keys[9], 71), 0),
        "tile_ids": touch_ends(jax.random.randint(arg_keys[7], (N_IMG, N_GS, TILE_DEV), 0, IMG_TILES * IMG_TILES), jax.random.fold_in(arg_keys[7], 1), 0, (IMG_TILES * IMG_TILES) - 1).astype(jnp.int32),
        "target": jnp.clip(1.0 * jax.random.uniform(arg_keys[8], (N_IMG, N_GS, TILE_DEV, 3, TILE * TILE), jnp.float32) ** steps_of(arg_keys[8], (N_IMG, N_GS, TILE_DEV, 3, TILE * TILE), ((0, 4), (1, 64)), -0.2, 0.2), 0.0, 1.0),
    }


sh_zero = 0.28209479177387814
sh_one = 0.4886025119029199
sh_two = (1.0925484305920792, -1.0925484305920792, 0.31539156525252005, -1.0925484305920792, 0.5462742152960396)
sh_three = (-0.5900435899266435, 2.890611442640554, -0.4570457994644658, 0.3731763325901154, -0.4570457994644658, 1.445305721320277, -0.5900435899266435)
learn_rates = np.array([0.00016] * 3 + [0.005] * 3 + [0.001] * 4 + [0.05] + [0.0025] * 3 + [0.000125] * 45)
bias_first = 1.0 - 0.9 ** 10
bias_second = 1.0 - 0.999 ** 10

def sh_basis(dir_x, dir_y, dir_z):
    square_x = dir_x * dir_x
    square_y = dir_y * dir_y
    square_z = dir_z * dir_z
    return [sh_zero * jnp.ones_like(dir_x), -sh_one * dir_y, sh_one * dir_z, -sh_one * dir_x, sh_two[0] * dir_x * dir_y, sh_two[1] * dir_y * dir_z, sh_two[2] * (2.0 * square_z - square_x - square_y), sh_two[3] * dir_x * dir_z, sh_two[4] * (square_x - square_y), sh_three[0] * dir_y * (3.0 * square_x - square_y), sh_three[1] * dir_x * dir_y * dir_z, sh_three[2] * dir_y * (4.0 * square_z - square_x - square_y), sh_three[3] * dir_z * (2.0 * square_z - 3.0 * square_x - 3.0 * square_y), sh_three[4] * dir_x * (4.0 * square_z - square_x - square_y), sh_three[5] * dir_z * (square_x - square_y), sh_three[6] * dir_x * (square_x - 3.0 * square_y)]

def project(raw, camera):
    world = [raw[0], raw[1], raw[2]]
    scales = [jnp.exp(raw[3]), jnp.exp(raw[4]), jnp.exp(raw[5])]
    quat_sq = jnp.maximum(raw[6] * raw[6] + raw[7] * raw[7] + raw[8] * raw[8] + raw[9] * raw[9], 0.25)
    inverse = lax.rsqrt(quat_sq)
    quat_w, quat_x, quat_y, quat_z = (raw[6] * inverse, raw[7] * inverse, raw[8] * inverse, raw[9] * inverse)
    rotation = [[1.0 - 2.0 * (quat_y * quat_y + quat_z * quat_z), 2.0 * (quat_x * quat_y - quat_w * quat_z), 2.0 * (quat_x * quat_z + quat_w * quat_y)], [2.0 * (quat_x * quat_y + quat_w * quat_z), 1.0 - 2.0 * (quat_x * quat_x + quat_z * quat_z), 2.0 * (quat_y * quat_z - quat_w * quat_x)], [2.0 * (quat_x * quat_z - quat_w * quat_y), 2.0 * (quat_y * quat_z + quat_w * quat_x), 1.0 - 2.0 * (quat_x * quat_x + quat_y * quat_y)]]
    spread = [[rotation[first][second] * scales[second] for second in range(3)] for first in range(3)]
    turn = [[camera[3 * first + second] for second in range(3)] for first in range(3)]
    viewed = [turn[first][0] * world[0] + turn[first][1] * world[1] + turn[first][2] * world[2] + camera[9 + first] for first in range(3)]
    inv_depth = 1.0 / viewed[2]
    focal = camera[15]
    jacobian = [[focal * inv_depth, 0.0 * inv_depth, -focal * viewed[0] * inv_depth * inv_depth], [0.0 * inv_depth, focal * inv_depth, -focal * viewed[1] * inv_depth * inv_depth]]
    screen = [[sum((jacobian[first][inner] * turn[inner][second] for inner in range(3))) for second in range(3)] for first in range(2)]
    mapped = [[sum((screen[first][inner] * spread[inner][second] for inner in range(3))) for second in range(3)] for first in range(2)]
    cov_xx = sum((mapped[0][inner] * mapped[0][inner] for inner in range(3))) + 0.3
    cov_xy = sum((mapped[0][inner] * mapped[1][inner] for inner in range(3)))
    cov_yy = sum((mapped[1][inner] * mapped[1][inner] for inner in range(3))) + 0.3
    determinant = cov_xx * cov_yy - cov_xy * cov_xy
    half_width = 0.5 * IMG_TILES * TILE
    ray = [world[first] - camera[12 + first] for first in range(3)]
    ray_scale = lax.rsqrt(ray[0] * ray[0] + ray[1] * ray[1] + ray[2] * ray[2])
    basis = sh_basis(ray[0] * ray_scale, ray[1] * ray_scale, ray[2] * ray_scale)
    colours = [jnp.maximum(sum((basis[term] * raw[11 + 3 * term + channel] for term in range(16))) + 0.5, 0.0) for channel in range(3)]
    return jnp.stack([focal * viewed[0] * inv_depth + half_width, focal * viewed[1] * inv_depth + half_width, cov_yy / determinant, -cov_xy / determinant, cov_xx / determinant, 0.99 * jax.nn.sigmoid(raw[10]), colours[0], colours[1], colours[2]])

def blend(features, live, pix_x, pix_y):
    offset_x = pix_x[:, :, None] - features[0][:, None, :]
    offset_y = pix_y[:, :, None] - features[1][:, None, :]
    power = -0.5 * (features[2][:, None, :] * offset_x * offset_x + 2.0 * features[3][:, None, :] * offset_x * offset_y + features[4][:, None, :] * offset_y * offset_y)
    alpha = features[5][:, None, :] * jnp.exp(power) * live[:, None, :]
    log_keep = jnp.log1p(-alpha)
    passed = jnp.exp(jnp.cumsum(log_keep, axis=-1) - log_keep)
    weight = passed * alpha
    return jnp.einsum('bps,cbs->bcp', weight, features[6:9], precision=lax.Precision.HIGHEST)

def render_tiles(features, slot_rows, tile_ids, target):
    tiles, slots = slot_rows.shape
    width = features.shape[0]
    live = slot_rows >= 0
    safe = jnp.where(live, slot_rows, 0).astype(jnp.int32)
    live_float = jnp.where(live, 1.0, 0.0).astype(features.dtype)
    gathered = jnp.take(features, safe.reshape(-1), axis=1).reshape(width, tiles, slots)
    lane = jnp.arange(TILE * TILE, dtype=jnp.int32)
    pix_x = (tile_ids[:, None] % IMG_TILES * TILE + lane[None, :] % TILE).astype(features.dtype) + 0.5
    pix_y = (tile_ids[:, None] // IMG_TILES * TILE + lane[None, :] // TILE).astype(features.dtype) + 0.5
    groups = tiles // 4
    stacked = (gathered.reshape(width, groups, 4, slots).transpose(1, 0, 2, 3), live_float.reshape(groups, 4, slots), pix_x.reshape(groups, 4, -1), pix_y.reshape(groups, 4, -1), target.reshape(groups, 4, 3, -1))

    def shade(block):
        feats_block, live_block, across, down, wanted = block
        colour, pull = jax.vjp(lambda part_feats: blend(part_feats, live_block, across, down), feats_block)
        slot_grad, = pull(colour - wanted)
        return (colour, slot_grad)
    colours, grads = lax.map(shade, stacked)
    slot_grads = grads.transpose(1, 0, 2, 3).reshape(width, tiles * slots)
    row_grads = jax.ops.segment_sum(slot_grads.T, safe.reshape(-1), num_segments=features.shape[1]).T
    return (colours.reshape(tiles, 3, -1), row_grads)

def adam_update(params, adam_m, adam_v, gradient):
    rates = jnp.asarray(learn_rates).astype(params.dtype)[:, None]
    new_m = 0.9 * adam_m + 0.1 * gradient
    new_v = 0.999 * adam_v + 0.001 * gradient * gradient
    new_params = params - rates * (new_m / bias_first) / (jnp.sqrt(new_v / bias_second) + 1e-08)
    return (new_params, new_m, new_v)

def reference(params, adam_m, adam_v, cameras, device_camera, send_index, slot_rows, tile_ids, target):
    n_img, n_gs = device_camera.shape
    g_dev = params.shape[1] // n_gs
    sources = jnp.arange(n_gs, dtype=jnp.int32)[:, None] * g_dev

    def device(gradient, flat):
        img_index = flat // n_gs
        gs_index = flat % n_gs
        rows = (sources + send_index[img_index, :, gs_index, :]).reshape(-1).astype(jnp.int32)
        camera = jnp.take(cameras, device_camera[img_index, gs_index][None], axis=1)
        features, pull = jax.vjp(lambda raw: project(raw, camera), jnp.take(params, rows, axis=1))
        colours, row_grads = render_tiles(features, slot_rows[img_index, gs_index], tile_ids[img_index, gs_index], target[img_index, gs_index])
        raw_grads, = pull(row_grads)
        return (gradient.at[:, rows].add(raw_grads), colours)
    gradient, colours = lax.scan(device, jnp.zeros(params.shape, jnp.float32), jnp.arange(n_img * n_gs, dtype=jnp.int32))
    new_params, new_m, new_v = adam_update(params, adam_m, adam_v, gradient)
    return (new_params, new_m, new_v, colours.reshape(target.shape))
```

```python
import jax
import jax.numpy as jnp
import numpy as np
from jax import lax
from jax.experimental import pallas as pl
from jax.experimental.pallas import tpu as pltpu
from jax.sharding import PartitionSpec as P

TILE = 16
IMG_TILES = 16


sh_zero = 0.28209479177387814
sh_one = 0.4886025119029199
sh_two = (
    1.0925484305920792,
    -1.0925484305920792,
    0.31539156525252005,
    -1.0925484305920792,
    0.5462742152960396,
)
sh_three = (
    -0.5900435899266435,
    2.890611442640554,
    -0.4570457994644658,
    0.3731763325901154,
    -0.4570457994644658,
    1.445305721320277,
    -0.5900435899266435,
)
learn_rates = np.array(
    [0.00016] * 3 + [0.005] * 3 + [0.001] * 4 + [0.05] + [0.0025] * 3 + [0.000125] * 45
)
bias_first = 1.0 - 0.9**10
bias_second = 1.0 - 0.999**10


def sh_basis(dir_x, dir_y, dir_z):
    square_x = dir_x * dir_x
    square_y = dir_y * dir_y
    square_z = dir_z * dir_z
    return [
        sh_zero * jnp.ones_like(dir_x),
        -sh_one * dir_y,
        sh_one * dir_z,
        -sh_one * dir_x,
        sh_two[0] * dir_x * dir_y,
        sh_two[1] * dir_y * dir_z,
        sh_two[2] * (2.0 * square_z - square_x - square_y),
        sh_two[3] * dir_x * dir_z,
        sh_two[4] * (square_x - square_y),
        sh_three[0] * dir_y * (3.0 * square_x - square_y),
        sh_three[1] * dir_x * dir_y * dir_z,
        sh_three[2] * dir_y * (4.0 * square_z - square_x - square_y),
        sh_three[3] * dir_z * (2.0 * square_z - 3.0 * square_x - 3.0 * square_y),
        sh_three[4] * dir_x * (4.0 * square_z - square_x - square_y),
        sh_three[5] * dir_z * (square_x - square_y),
        sh_three[6] * dir_x * (square_x - 3.0 * square_y),
    ]


def project(raw, camera):
    world = [raw[0], raw[1], raw[2]]
    scales = [jnp.exp(raw[3]), jnp.exp(raw[4]), jnp.exp(raw[5])]
    quat_sq = jnp.maximum(
        raw[6] * raw[6] + raw[7] * raw[7] + raw[8] * raw[8] + raw[9] * raw[9], 0.25
    )
    inverse = lax.rsqrt(quat_sq)
    quat_w, quat_x, quat_y, quat_z = (
        raw[6] * inverse,
        raw[7] * inverse,
        raw[8] * inverse,
        raw[9] * inverse,
    )
    rotation = [
        [
            1.0 - 2.0 * (quat_y * quat_y + quat_z * quat_z),
            2.0 * (quat_x * quat_y - quat_w * quat_z),
            2.0 * (quat_x * quat_z + quat_w * quat_y),
        ],
        [
            2.0 * (quat_x * quat_y + quat_w * quat_z),
            1.0 - 2.0 * (quat_x * quat_x + quat_z * quat_z),
            2.0 * (quat_y * quat_z - quat_w * quat_x),
        ],
        [
            2.0 * (quat_x * quat_z - quat_w * quat_y),
            2.0 * (quat_y * quat_z + quat_w * quat_x),
            1.0 - 2.0 * (quat_x * quat_x + quat_y * quat_y),
        ],
    ]
    spread = [
        [rotation[first][second] * scales[second] for second in range(3)] for first in range(3)
    ]
    turn = [[camera[3 * first + second] for second in range(3)] for first in range(3)]
    viewed = [
        turn[first][0] * world[0]
        + turn[first][1] * world[1]
        + turn[first][2] * world[2]
        + camera[9 + first]
        for first in range(3)
    ]
    inv_depth = 1.0 / viewed[2]
    focal = camera[15]
    jacobian = [
        [focal * inv_depth, 0.0 * inv_depth, -focal * viewed[0] * inv_depth * inv_depth],
        [0.0 * inv_depth, focal * inv_depth, -focal * viewed[1] * inv_depth * inv_depth],
    ]
    screen = [
        [
            sum((jacobian[first][inner] * turn[inner][second] for inner in range(3)))
            for second in range(3)
        ]
        for first in range(2)
    ]
    mapped = [
        [
            sum((screen[first][inner] * spread[inner][second] for inner in range(3)))
            for second in range(3)
        ]
        for first in range(2)
    ]
    cov_xx = sum((mapped[0][inner] * mapped[0][inner] for inner in range(3))) + 0.3
    cov_xy = sum((mapped[0][inner] * mapped[1][inner] for inner in range(3)))
    cov_yy = sum((mapped[1][inner] * mapped[1][inner] for inner in range(3))) + 0.3
    determinant = cov_xx * cov_yy - cov_xy * cov_xy
    half_width = 0.5 * IMG_TILES * TILE
    ray = [world[first] - camera[12 + first] for first in range(3)]
    ray_scale = lax.rsqrt(ray[0] * ray[0] + ray[1] * ray[1] + ray[2] * ray[2])
    basis = sh_basis(ray[0] * ray_scale, ray[1] * ray_scale, ray[2] * ray_scale)
    colours = [
        jnp.maximum(
            sum((basis[term] * raw[11 + 3 * term + channel] for term in range(16))) + 0.5, 0.0
        )
        for channel in range(3)
    ]
    return jnp.stack(
        [
            focal * viewed[0] * inv_depth + half_width,
            focal * viewed[1] * inv_depth + half_width,
            cov_yy / determinant,
            -cov_xy / determinant,
            cov_xx / determinant,
            0.99 * jax.nn.sigmoid(raw[10]),
            colours[0],
            colours[1],
            colours[2],
        ]
    )


F32, BF16, I32 = jnp.float32, jnp.bfloat16, jnp.int32
NN = (((1,), (0,)), ((), ()))
NT = (((1,), (1,)), ((), ()))
LN2 = float(np.log(2.0))


def dot(left, right, dims=NN):
    return lax.dot_general(left, right, dims, preferred_element_type=F32)


def split2(value):
    high = value.astype(BF16)
    return high, (value - high.astype(F32)).astype(BF16)


def split3(value):
    high = value.astype(BF16)
    rest = value - high.astype(F32)
    mid = rest.astype(BF16)
    return high, mid, (rest - mid.astype(F32)).astype(BF16)


def iota(shape, dim):
    return lax.broadcasted_iota(I32, shape, dim)


def render_kernel(
    tid_ref, recv_ref, slots_ref, target_ref, colour_ref, out_ref,
    table, onehot, coef, power_w, diff_w, alpha, weight, weight_h, weight_l, pull,
    dp_h, dp_m, dp_l, spread, total, mono,
):
    groups, _, rows = slots_ref.shape
    slots = rows // 8
    for feat in range(9):
        block = jnp.concatenate(
            [recv_ref[16 * j : 16 * j + 16, 64 * feat : 64 * feat + 64] for j in range(4)], axis=1
        )
        for part, piece in enumerate(split3(block)):
            table[pl.ds((part * 9 + feat) * 16, 16), :] = piece
    total[...] = jnp.zeros_like(total)
    coef[...] = jnp.zeros_like(coef)
    diff_w[...] = jnp.zeros_like(diff_w)
    pixel = iota((16, 256), 1)
    off_u = (pixel & 15).astype(F32) - 7.5
    off_v = (pixel >> 4).astype(F32) - 7.5
    which = iota((16, 256), 0)
    def pick(kind, u, v):
        out = jnp.where(kind == 0, 1.0, 0.0)
        out = jnp.where(kind == 1, u, out)
        out = jnp.where(kind == 2, v, out)
        out = jnp.where(kind == 3, u * u, out)
        out = jnp.where(kind == 4, u * v, out)
        return jnp.where(kind == 5, v * v, out)
    mono[...] = pick(which, off_u, off_v).astype(BF16)
    row = iota((128, 256), 0)
    pix = iota((128, 256), 1)
    kind = jnp.where(row >= 12, row - 12, jnp.where(row >= 6, row - 6, row))
    power_w[...] = jnp.where(
        row < 18,
        pick(kind, (pix & 15).astype(F32) - 7.5, (pix >> 4).astype(F32) - 7.5),
        0.0,
    ).astype(BF16)

    lane_tile = iota((1, rows), 1) & 7
    own = iota((8, rows), 0) == lane_tile
    hi_row = iota((16, rows), 0)

    def group(step, carry):
        index = slots_ref[step]
        live = index >= 0
        low = ((index >> 10) << 6) | (index & 63)
        high = jnp.where(live, (index >> 6) & 15, -1)
        onehot[...] = jnp.where(iota((256, rows), 0) == low, 1.0, 0.0).astype(BF16)
        mask = hi_row == high
        raw = dot(table[...], onehot[...])
        feats = []
        for feat in range(9):
            part = (
                raw[288 + 16 * feat : 304 + 16 * feat] + raw[144 + 16 * feat : 160 + 16 * feat]
            ) + raw[16 * feat : 16 * feat + 16]
            feats.append(jnp.sum(jnp.where(mask, part, 0.0), axis=0, keepdims=True))
        mean_x, mean_y, con_a, con_b, con_c, log_op = feats[:6]
        centre_x = jnp.zeros((1, rows), F32)
        centre_y = jnp.zeros((1, rows), F32)
        for t in range(8):
            tid = tid_ref[0, step * 8 + t]
            centre_x = jnp.where(lane_tile == t, ((tid & 15) * 16 + 8).astype(F32), centre_x)
            centre_y = jnp.where(lane_tile == t, ((tid >> 4) * 16 + 8).astype(F32), centre_y)
        far_x = centre_x - mean_x
        far_y = centre_y - mean_y
        ax = con_a * far_x
        bx = con_b * far_x
        by = con_b * far_y
        cy = con_c * far_y
        constant = far_x * (ax + by) + far_y * cy + log_op
        constant = jnp.where(live, constant, -1e30)
        for m, value in enumerate(
            (constant, 2.0 * ax + by, bx + 2.0 * cy, con_a, con_b, con_c)
        ):
            for part, piece in enumerate(split3(value)):
                coef[pl.ds(part * 6 + m, 1), :] = piece.astype(F32)
        for ch in range(3):
            c_high, c_mid = split2(feats[6 + ch])
            c_high = jnp.where(own, c_high.astype(F32), 0.0)
            coef[24 + 8 * ch : 32 + 8 * ch, :] = c_high
            coef[48 + 8 * ch : 56 + 8 * ch, :] = jnp.where(own, c_mid.astype(F32), 0.0)
            coef[72 + 8 * ch : 80 + 8 * ch, :] = c_high
        turned = jnp.transpose(coef[...]).astype(BF16)
        alpha[...] = dot(turned, power_w[...])

        def forward(chunk, passed):
            base = pl.multiple_of(chunk * 128, 128)
            powers = alpha[pl.ds(base, 128), :]
            alphas = jnp.exp2(powers)
            alpha[pl.ds(base, 128), :] = alphas
            out = []
            for k in range(16):
                w = passed * alphas[8 * k : 8 * k + 8]
                passed = passed - w
                out.append(w)
            out = jnp.concatenate(out, axis=0)
            weight[pl.ds(base, 128), :] = out
            w_h, w_l = split2(out)
            weight_h[pl.ds(base, 128), :] = w_h
            weight_l[pl.ds(base, 128), :] = w_l
            return passed

        lax.fori_loop(0, slots // 16, forward, jnp.ones((8, 256), F32))
        tinted = coef[24:72, :].astype(BF16)
        first = dot(tinted, weight_h[...])
        second = dot(tinted, weight_l[...])
        shown = first[:24] + (first[24:48] + second[:24])
        diffs_h, diffs_m = [], []
        for ch in range(3):
            colour = shown[8 * ch : 8 * ch + 8]
            where = pl.ds(pl.multiple_of(step * 8, 8), 8)
            colour_ref[ch, where, :] = colour
            d_high, d_mid = split2(colour - target_ref[ch, where, :])
            d_high = d_high.astype(F32)
            diffs_h.append(d_high)
            diffs_m.append(d_mid.astype(F32))
            diff_w[24 + 8 * ch : 32 + 8 * ch, :] = d_high
            diff_w[48 + 8 * ch : 56 + 8 * ch, :] = d_high
            diff_w[72 + 8 * ch : 80 + 8 * ch, :] = d_mid.astype(F32)
        pull[...] = dot(turned, diff_w[...].astype(BF16))

        def backward(chunk, behind):
            base = pl.multiple_of((slots // 16 - 1 - chunk) * 128, 128)
            alphas = alpha[pl.ds(base, 128), :]
            weights = weight[pl.ds(base, 128), :]
            pulls = pull[pl.ds(base, 128), :]
            out = [None] * 16
            for k in range(15, -1, -1):
                gap = pulls[8 * k : 8 * k + 8] - behind
                out[k] = weights[8 * k : 8 * k + 8] * gap
                behind = behind + alphas[8 * k : 8 * k + 8] * gap
            out = jnp.concatenate(out, axis=0)
            d_h, d_m, d_l = split3(out)
            dp_h[pl.ds(base, 128), :] = d_h
            dp_m[pl.ds(base, 128), :] = d_m
            dp_l[pl.ds(base, 128), :] = d_l
            return behind

        lax.fori_loop(0, slots // 16, backward, jnp.zeros((8, 256), F32))
        diff48 = diff_w[48:96, :].astype(BF16)
        tint_h = dot(diff48, weight_h[...], NT)
        tint_l = dot(diff48, weight_l[...], NT)
        tint = tint_h[:24] + (tint_h[24:48] + tint_l[:24])
        moments = (
            dot(mono[...], dp_l[...], NT) + dot(mono[...], dp_m[...], NT)
        ) + dot(mono[...], dp_h[...], NT)
        s_0, s_u, s_v, s_uu, s_uv, s_vv = [LN2 * moments[m : m + 1] for m in range(6)]
        sum_x = far_x * s_0 + s_u
        sum_y = far_y * s_0 + s_v
        grads = [
            -(2.0 * con_a * sum_x + con_b * sum_y),
            -(con_b * sum_x + 2.0 * con_c * sum_y),
            far_x * (sum_x + s_u) + s_uu,
            far_x * sum_y + far_y * s_u + s_uv,
            far_y * (sum_y + s_v) + s_vv,
            s_0,
        ] + [
            jnp.sum(jnp.where(own, tint[8 * ch : 8 * ch + 8], 0.0), axis=0, keepdims=True)
            for ch in range(3)
        ]
        for feat in range(9):
            for part, piece in enumerate(split3(grads[feat])):
                spread[pl.ds((part * 9 + feat) * 16, 16), :] = jnp.where(
                    mask, piece.astype(F32), 0.0
                ).astype(BF16)
        total[...] += dot(spread[...], onehot[...], NT)
        return carry

    lax.fori_loop(0, groups, group, 0)
    for feat in range(9):
        grid = (
            total[16 * feat + 288 : 16 * feat + 304] + total[16 * feat + 144 : 16 * feat + 160]
        ) + total[16 * feat : 16 * feat + 16]
        for j in range(4):
            out_ref[16 * j : 16 * j + 16, 64 * feat : 64 * feat + 64] = grid[
                :, 64 * j : 64 * j + 64
            ]
    out_ref[:, 576:640] = jnp.zeros((64, 64), F32)


def render(recv, slot_rows, tile_ids, target):
    tiles, slots = slot_rows.shape
    groups = tiles // 8
    rows = slots * 8
    ordered = slot_rows.reshape(groups, 8, slots).transpose(0, 2, 1).reshape(groups, 1, rows)
    vm = lambda *shape_type: pltpu.VMEM(*shape_type)
    return pl.pallas_call(
        render_kernel,
        out_shape=(
            jax.ShapeDtypeStruct((3, tiles, 256), F32),
            jax.ShapeDtypeStruct((64, 640), F32),
        ),
        in_specs=[
            pl.BlockSpec(memory_space=pltpu.SMEM),
            pl.BlockSpec(memory_space=pltpu.VMEM),
            pl.BlockSpec(memory_space=pltpu.VMEM),
            pl.BlockSpec(memory_space=pltpu.VMEM),
        ],
        out_specs=(
            pl.BlockSpec(memory_space=pltpu.VMEM),
            pl.BlockSpec(memory_space=pltpu.VMEM),
        ),
        scratch_shapes=[
            vm((432, 256), BF16),
            vm((256, rows), BF16),
            vm((128, rows), F32),
            vm((128, 256), BF16),
            vm((128, 256), F32),
            vm((rows, 256), F32),
            vm((rows, 256), F32),
            vm((rows, 256), BF16),
            vm((rows, 256), BF16),
            vm((rows, 256), F32),
            vm((rows, 256), BF16),
            vm((rows, 256), BF16),
            vm((rows, 256), BF16),
            vm((432, rows), BF16),
            vm((432, 256), F32),
            vm((16, 256), BF16),
        ],
        compiler_params=pltpu.CompilerParams(vmem_limit_bytes=56 * 1024 * 1024),
        name="render",
    )(tile_ids, recv, ordered, target)


def adam_update(params, adam_m, adam_v, gradient):
    rates = jnp.asarray(learn_rates, jnp.float32)[:, None]
    new_m = 0.9 * adam_m + 0.1 * gradient
    new_v = 0.999 * adam_v + 0.001 * gradient * gradient
    new_params = params - rates * (new_m / bias_first) / (jnp.sqrt(new_v / bias_second) + 1e-08)
    return (new_params, new_m, new_v)


def sent_features(raw, camera):
    feats = project(raw, camera)
    log2_e = 1.0 / LN2
    return jnp.stack(
        [
            feats[0],
            feats[1],
            (-0.5 * log2_e) * feats[2],
            -log2_e * feats[3],
            (-0.5 * log2_e) * feats[4],
            jnp.log(feats[5]) * log2_e,
            feats[6],
            feats[7],
            feats[8],
        ]
    )


def on_device(
    params, adam_m, adam_v, cameras, device_camera, send_index, slot_rows, tile_ids, target
):
    local = send_index[0, 0].reshape(-1)
    raw = jnp.take(params, local, axis=1).reshape(-1, 32, 128)
    dest_cameras = jnp.take(cameras, device_camera[0], axis=1)
    camera = jnp.repeat(dest_cameras, 64, axis=1).reshape(16, 32, 128)
    features, pull = jax.vjp(lambda rows: sent_features(rows, camera), raw)
    outgoing = features.reshape(9, 64, 64).transpose(1, 0, 2).reshape(64, 576)
    incoming = lax.all_to_all(outgoing, "gs", 0, 0, tiled=True)
    colours, back = render(
        jnp.pad(incoming, ((0, 0), (0, 64))),
        slot_rows[0, 0],
        tile_ids[0],
        target[0, 0].transpose(1, 0, 2),
    )
    returned = lax.all_to_all(back[:, :576], "gs", 0, 0, tiled=True)
    (raw_grads,) = pull(returned.reshape(64, 9, 64).transpose(1, 0, 2).reshape(9, 32, 128))
    gradient = jax.ops.segment_sum(
        raw_grads.reshape(59, -1).T, local, num_segments=params.shape[1]
    ).T
    total = lax.psum(gradient, "img")
    new_params, new_m, new_v = adam_update(params, adam_m, adam_v, total)
    return (new_params, new_m, new_v, colours.transpose(1, 0, 2)[None, None])


def solution(mesh):
    return jax.shard_map(
        on_device,
        mesh=mesh,
        in_specs=(
            P(None, "gs"),
            P(None, "gs"),
            P(None, "gs"),
            P(),
            P("img", None),
            P("img", "gs", None, None),
            P("img", "gs", None, None),
            P("img", "gs", None),
            P("img", "gs", None, None, None),
        ),
        out_specs=(P(None, "gs"), P(None, "gs"), P(None, "gs"), P("img", "gs", None, None, None)),
        check_vma=False,
    )
```

```python
import jax
import jax.numpy as jnp
import numpy as np
from jax import lax
from jax.experimental import pallas as pl
from jax.experimental.pallas import tpu as pltpu
from jax.sharding import PartitionSpec as P

TILE = 16
IMG_TILES = 16


sh_zero = 0.28209479177387814
sh_one = 0.4886025119029199
sh_two = (
    1.0925484305920792,
    -1.0925484305920792,
    0.31539156525252005,
    -1.0925484305920792,
    0.5462742152960396,
)
sh_three = (
    -0.5900435899266435,
    2.890611442640554,
    -0.4570457994644658,
    0.3731763325901154,
    -0.4570457994644658,
    1.445305721320277,
    -0.5900435899266435,
)
learn_rates = np.array(
    [0.00016] * 3 + [0.005] * 3 + [0.001] * 4 + [0.05] + [0.0025] * 3 + [0.000125] * 45
)
LN2 = float(np.log(2.0))
LOG2_E = 1.0 / LN2
LOG_TOP = float(np.log2(0.99))
bias_first = 1.0 - 0.9**10
bias_second = 1.0 - 0.999**10


def sh_basis(dir_x, dir_y, dir_z):
    square_x = dir_x * dir_x
    square_y = dir_y * dir_y
    square_z = dir_z * dir_z
    return [
        sh_zero * jnp.ones_like(dir_x),
        -sh_one * dir_y,
        sh_one * dir_z,
        -sh_one * dir_x,
        sh_two[0] * dir_x * dir_y,
        sh_two[1] * dir_y * dir_z,
        sh_two[2] * (2.0 * square_z - square_x - square_y),
        sh_two[3] * dir_x * dir_z,
        sh_two[4] * (square_x - square_y),
        sh_three[0] * dir_y * (3.0 * square_x - square_y),
        sh_three[1] * dir_x * dir_y * dir_z,
        sh_three[2] * dir_y * (4.0 * square_z - square_x - square_y),
        sh_three[3] * dir_z * (2.0 * square_z - 3.0 * square_x - 3.0 * square_y),
        sh_three[4] * dir_x * (4.0 * square_z - square_x - square_y),
        sh_three[5] * dir_z * (square_x - square_y),
        sh_three[6] * dir_x * (square_x - 3.0 * square_y),
    ]


def sent_features(raw, camera):
    world = [raw[0], raw[1], raw[2]]
    scales = [jnp.exp(raw[3]), jnp.exp(raw[4]), jnp.exp(raw[5])]
    quat_sq = jnp.maximum(
        raw[6] * raw[6] + raw[7] * raw[7] + raw[8] * raw[8] + raw[9] * raw[9], 0.25
    )
    inverse = lax.rsqrt(quat_sq)
    quat_w, quat_x, quat_y, quat_z = (
        raw[6] * inverse,
        raw[7] * inverse,
        raw[8] * inverse,
        raw[9] * inverse,
    )
    rotation = [
        [
            1.0 - 2.0 * (quat_y * quat_y + quat_z * quat_z),
            2.0 * (quat_x * quat_y - quat_w * quat_z),
            2.0 * (quat_x * quat_z + quat_w * quat_y),
        ],
        [
            2.0 * (quat_x * quat_y + quat_w * quat_z),
            1.0 - 2.0 * (quat_x * quat_x + quat_z * quat_z),
            2.0 * (quat_y * quat_z - quat_w * quat_x),
        ],
        [
            2.0 * (quat_x * quat_z - quat_w * quat_y),
            2.0 * (quat_y * quat_z + quat_w * quat_x),
            1.0 - 2.0 * (quat_x * quat_x + quat_y * quat_y),
        ],
    ]
    spread = [
        [rotation[first][second] * scales[second] for second in range(3)] for first in range(3)
    ]
    turn = [[camera[3 * first + second] for second in range(3)] for first in range(3)]
    viewed = [
        turn[first][0] * world[0]
        + turn[first][1] * world[1]
        + turn[first][2] * world[2]
        + camera[9 + first]
        for first in range(3)
    ]
    inv_depth = 1.0 / viewed[2]
    focal = camera[15]
    jacobian = [
        [focal * inv_depth, 0.0 * inv_depth, -focal * viewed[0] * inv_depth * inv_depth],
        [0.0 * inv_depth, focal * inv_depth, -focal * viewed[1] * inv_depth * inv_depth],
    ]
    screen = [
        [
            sum((jacobian[first][inner] * turn[inner][second] for inner in range(3)))
            for second in range(3)
        ]
        for first in range(2)
    ]
    mapped = [
        [
            sum((screen[first][inner] * spread[inner][second] for inner in range(3)))
            for second in range(3)
        ]
        for first in range(2)
    ]
    cov_xx = sum((mapped[0][inner] * mapped[0][inner] for inner in range(3))) + 0.3
    cov_xy = sum((mapped[0][inner] * mapped[1][inner] for inner in range(3)))
    cov_yy = sum((mapped[1][inner] * mapped[1][inner] for inner in range(3))) + 0.3
    determinant = cov_xx * cov_yy - cov_xy * cov_xy
    half_width = 0.5 * IMG_TILES * TILE
    ray = [world[first] - camera[12 + first] for first in range(3)]
    ray_scale = lax.rsqrt(ray[0] * ray[0] + ray[1] * ray[1] + ray[2] * ray[2])
    basis = sh_basis(ray[0] * ray_scale, ray[1] * ray_scale, ray[2] * ray_scale)
    colours = [
        jnp.maximum(
            sum((basis[term] * raw[11 + 3 * term + channel] for term in range(16))) + 0.5, 0.0
        )
        for channel in range(3)
    ]
    inverse_det = 1.0 / determinant
    log_opacity = LOG_TOP - jnp.log(1.0 + jnp.exp(-raw[10])) * LOG2_E
    return [
        focal * viewed[0] * inv_depth + half_width,
        focal * viewed[1] * inv_depth + half_width,
        (-0.5 * LOG2_E) * cov_yy * inverse_det,
        LOG2_E * cov_xy * inverse_det,
        (-0.5 * LOG2_E) * cov_xx * inverse_det,
        log_opacity,
        colours[0],
        colours[1],
        colours[2],
    ]


F32, BF16, I32 = jnp.float32, jnp.bfloat16, jnp.int32
NN = (((1,), (0,)), ((), ()))
NT = (((1,), (1,)), ((), ()))


def dot(left, right, dims=NN):
    return lax.dot_general(left, right, dims, preferred_element_type=F32)


def split2(value):
    high = value.astype(BF16)
    return high, (value - high.astype(F32)).astype(BF16)


def split3(value):
    high = value.astype(BF16)
    rest = value - high.astype(F32)
    mid = rest.astype(BF16)
    return high, mid, (rest - mid.astype(F32)).astype(BF16)


def iota(shape, dim):
    return lax.broadcasted_iota(I32, shape, dim)


def render_kernel(
    tid_ref, recv_ref, slots_ref, target_ref, colour_ref, out_ref,
    table, onehot, coef, power_w, diff_w, alpha, weight, weight_h, weight_l, pull,
    dp_h, dp_m, dp_l, spread, total, mono,
):
    groups, _, rows = slots_ref.shape
    slots = rows // 8
    for feat in range(9):
        side = slice(64 * (feat % 2), 64 * (feat % 2) + 64)
        block = jnp.concatenate(
            [recv_ref[pl.ds(80 * j + feat // 2, 16, stride=5), :][:, side] for j in range(4)],
            axis=1,
        )
        for part, piece in enumerate(split3(block)):
            table[pl.ds((part * 9 + feat) * 16, 16), :] = piece
    total[...] = jnp.zeros_like(total)
    coef[...] = jnp.zeros_like(coef)
    diff_w[...] = jnp.zeros_like(diff_w)
    pixel = iota((16, 256), 1)
    off_u = (pixel & 15).astype(F32) - 7.5
    off_v = (pixel >> 4).astype(F32) - 7.5
    which = iota((16, 256), 0)
    def pick(kind, u, v):
        out = jnp.where(kind == 0, 1.0, 0.0)
        out = jnp.where(kind == 1, u, out)
        out = jnp.where(kind == 2, v, out)
        out = jnp.where(kind == 3, u * u, out)
        out = jnp.where(kind == 4, u * v, out)
        return jnp.where(kind == 5, v * v, out)
    mono[...] = pick(which, off_u, off_v).astype(BF16)
    row = iota((128, 256), 0)
    pix = iota((128, 256), 1)
    kind = jnp.where(row >= 12, row - 12, jnp.where(row >= 6, row - 6, row))
    power_w[...] = jnp.where(
        row < 18,
        pick(kind, (pix & 15).astype(F32) - 7.5, (pix >> 4).astype(F32) - 7.5),
        0.0,
    ).astype(BF16)

    lane_tile = iota((1, rows), 1) & 7
    own = iota((8, rows), 0) == lane_tile
    hi_row = iota((16, rows), 0)

    def group(step, carry):
        index = slots_ref[step]
        live = index >= 0
        low = ((index >> 10) << 6) | (index & 63)
        high = jnp.where(live, (index >> 6) & 15, -1)
        onehot[...] = jnp.where(iota((256, rows), 0) == low, 1.0, 0.0).astype(BF16)
        mask = hi_row == high
        raw = dot(table[...], onehot[...])
        feats = []
        for feat in range(9):
            part = (
                raw[288 + 16 * feat : 304 + 16 * feat] + raw[144 + 16 * feat : 160 + 16 * feat]
            ) + raw[16 * feat : 16 * feat + 16]
            feats.append(jnp.sum(jnp.where(mask, part, 0.0), axis=0, keepdims=True))
        mean_x, mean_y, con_a, con_b, con_c, log_op = feats[:6]
        centre_x = jnp.zeros((1, rows), F32)
        centre_y = jnp.zeros((1, rows), F32)
        for t in range(8):
            tid = tid_ref[0, step * 8 + t]
            centre_x = jnp.where(lane_tile == t, ((tid & 15) * 16 + 8).astype(F32), centre_x)
            centre_y = jnp.where(lane_tile == t, ((tid >> 4) * 16 + 8).astype(F32), centre_y)
        far_x = centre_x - mean_x
        far_y = centre_y - mean_y
        ax = con_a * far_x
        bx = con_b * far_x
        by = con_b * far_y
        cy = con_c * far_y
        constant = far_x * (ax + by) + far_y * cy + log_op
        constant = jnp.where(live, constant, -1e30)
        for m, value in enumerate(
            (constant, 2.0 * ax + by, bx + 2.0 * cy, con_a, con_b, con_c)
        ):
            for part, piece in enumerate(split3(value)):
                coef[pl.ds(part * 6 + m, 1), :] = piece.astype(F32)
        for ch in range(3):
            c_high, c_mid = split2(feats[6 + ch])
            c_high = jnp.where(own, c_high.astype(F32), 0.0)
            coef[24 + 8 * ch : 32 + 8 * ch, :] = c_high
            coef[48 + 8 * ch : 56 + 8 * ch, :] = jnp.where(own, c_mid.astype(F32), 0.0)
            coef[72 + 8 * ch : 80 + 8 * ch, :] = c_high
        turned = jnp.transpose(coef[...]).astype(BF16)
        alpha[...] = dot(turned, power_w[...])

        def forward(chunk, passed):
            base = pl.multiple_of(chunk * 128, 128)
            powers = alpha[pl.ds(base, 128), :]
            alphas = jnp.exp2(powers)
            alpha[pl.ds(base, 128), :] = alphas
            out = []
            for k in range(16):
                w = passed * alphas[8 * k : 8 * k + 8]
                passed = passed - w
                out.append(w)
            out = jnp.concatenate(out, axis=0)
            weight[pl.ds(base, 128), :] = out
            w_h, w_l = split2(out)
            weight_h[pl.ds(base, 128), :] = w_h
            weight_l[pl.ds(base, 128), :] = w_l
            return passed

        lax.fori_loop(0, slots // 16, forward, jnp.ones((8, 256), F32))
        tinted = coef[24:72, :].astype(BF16)
        first = dot(tinted, weight_h[...])
        second = dot(tinted, weight_l[...])
        shown = first[:24] + (first[24:48] + second[:24])
        diffs_h, diffs_m = [], []
        for ch in range(3):
            colour = shown[8 * ch : 8 * ch + 8]
            where = pl.ds(pl.multiple_of(step * 8, 8), 8)
            colour_ref[ch, where, :] = colour
            d_high, d_mid = split2(colour - target_ref[ch, where, :])
            d_high = d_high.astype(F32)
            diffs_h.append(d_high)
            diffs_m.append(d_mid.astype(F32))
            diff_w[24 + 8 * ch : 32 + 8 * ch, :] = d_high
            diff_w[48 + 8 * ch : 56 + 8 * ch, :] = d_high
            diff_w[72 + 8 * ch : 80 + 8 * ch, :] = d_mid.astype(F32)
        pull[...] = dot(turned, diff_w[...].astype(BF16))

        def backward(chunk, behind):
            base = pl.multiple_of((slots // 16 - 1 - chunk) * 128, 128)
            alphas = alpha[pl.ds(base, 128), :]
            weights = weight[pl.ds(base, 128), :]
            pulls = pull[pl.ds(base, 128), :]
            out = [None] * 16
            for k in range(15, -1, -1):
                gap = pulls[8 * k : 8 * k + 8] - behind
                out[k] = weights[8 * k : 8 * k + 8] * gap
                behind = behind + alphas[8 * k : 8 * k + 8] * gap
            out = jnp.concatenate(out, axis=0)
            d_h, d_m, d_l = split3(out)
            dp_h[pl.ds(base, 128), :] = d_h
            dp_m[pl.ds(base, 128), :] = d_m
            dp_l[pl.ds(base, 128), :] = d_l
            return behind

        lax.fori_loop(0, slots // 16, backward, jnp.zeros((8, 256), F32))
        diff48 = diff_w[48:96, :].astype(BF16)
        tint_h = dot(diff48, weight_h[...], NT)
        tint_l = dot(diff48, weight_l[...], NT)
        tint = tint_h[:24] + (tint_h[24:48] + tint_l[:24])
        moments = (
            dot(mono[...], dp_l[...], NT) + dot(mono[...], dp_m[...], NT)
        ) + dot(mono[...], dp_h[...], NT)
        s_0, s_u, s_v, s_uu, s_uv, s_vv = [LN2 * moments[m : m + 1] for m in range(6)]
        sum_x = far_x * s_0 + s_u
        sum_y = far_y * s_0 + s_v
        grads = [
            -(2.0 * con_a * sum_x + con_b * sum_y),
            -(con_b * sum_x + 2.0 * con_c * sum_y),
            far_x * (sum_x + s_u) + s_uu,
            far_x * sum_y + far_y * s_u + s_uv,
            far_y * (sum_y + s_v) + s_vv,
            s_0,
        ] + [
            jnp.sum(jnp.where(own, tint[8 * ch : 8 * ch + 8], 0.0), axis=0, keepdims=True)
            for ch in range(3)
        ]
        for feat in range(9):
            for part, piece in enumerate(split3(grads[feat])):
                spread[pl.ds((part * 9 + feat) * 16, 16), :] = jnp.where(
                    mask, piece.astype(F32), 0.0
                ).astype(BF16)
        total[...] += dot(spread[...], onehot[...], NT)
        return carry

    lax.fori_loop(0, groups, group, 0)
    grids = []
    for feat in range(9):
        grids.append(
            (total[16 * feat + 288 : 16 * feat + 304] + total[16 * feat + 144 : 16 * feat + 160])
            + total[16 * feat : 16 * feat + 16]
        )
    grids.append(jnp.zeros((16, 256), F32))
    for pair in range(5):
        for j in range(4):
            lanes = slice(64 * j, 64 * j + 64)
            out_ref[pl.ds(80 * j + pair, 16, stride=5), :] = jnp.concatenate(
                [grids[2 * pair][:, lanes], grids[2 * pair + 1][:, lanes]], axis=1
            )


def render(recv, slot_rows, tile_ids, target):
    tiles, slots = slot_rows.shape
    groups = tiles // 8
    rows = slots * 8
    ordered = slot_rows.reshape(groups, 8, slots).transpose(0, 2, 1).reshape(groups, 1, rows)
    vm = lambda *shape_type: pltpu.VMEM(*shape_type)
    return pl.pallas_call(
        render_kernel,
        out_shape=(
            jax.ShapeDtypeStruct((3, tiles, 256), F32),
            jax.ShapeDtypeStruct((320, 128), F32),
        ),
        in_specs=[
            pl.BlockSpec(memory_space=pltpu.SMEM),
            pl.BlockSpec(memory_space=pltpu.VMEM),
            pl.BlockSpec(memory_space=pltpu.VMEM),
            pl.BlockSpec(memory_space=pltpu.VMEM),
        ],
        out_specs=(
            pl.BlockSpec(memory_space=pltpu.VMEM),
            pl.BlockSpec(memory_space=pltpu.VMEM),
        ),
        scratch_shapes=[
            vm((432, 256), BF16),
            vm((256, rows), BF16),
            vm((128, rows), F32),
            vm((128, 256), BF16),
            vm((128, 256), F32),
            vm((rows, 256), F32),
            vm((rows, 256), F32),
            vm((rows, 256), BF16),
            vm((rows, 256), BF16),
            vm((rows, 256), F32),
            vm((rows, 256), BF16),
            vm((rows, 256), BF16),
            vm((rows, 256), BF16),
            vm((432, rows), BF16),
            vm((432, 256), F32),
            vm((16, 256), BF16),
        ],
        compiler_params=pltpu.CompilerParams(vmem_limit_bytes=56 * 1024 * 1024),
        name="render",
    )(tile_ids, recv, ordered, target)


def camera_block(camera_ref, chosen_ref, block):
    lane = iota((8, 128), 1)
    sub = iota((8, 128), 0)
    which = jnp.zeros((8, 128), I32)
    for k in range(8):
        near = chosen_ref[0, block * 8 + k]
        far = chosen_ref[0, 32 + block * 8 + k]
        which = jnp.where(sub == k, jnp.where(lane < 64, near, far), which)
    values = [jnp.zeros((8, 128), F32) for _ in range(16)]
    for cam in range(16):
        here = which == cam
        values = [
            jnp.where(here, camera_ref[k, cam], value) for k, value in enumerate(values)
        ]
    return values


def row_index(send_ref, index):
    index[...] = jnp.concatenate([send_ref[:32, :], send_ref[32:, :]], axis=1)


def send_kernel(camera_ref, chosen_ref, send_ref, params_ref, out_ref, raw_ref, table, index, feats):
    row_index(send_ref, index)
    for hi in range(8):
        piece = params_ref[:, 512 * hi : 512 * hi + 512]
        piece = jnp.concatenate([piece, jnp.zeros((5, 512), F32)], axis=0)
        high, mid, low = split3(piece)
        table[144 * hi : 144 * hi + 64, :] = high
        table[144 * hi + 64 : 144 * hi + 128, :] = mid
        table[144 * hi + 128 : 144 * hi + 144, :] = low[:16]

    def pick(block, carry):
        here = jnp.concatenate(
            [index[pl.ds(2 * block, 1), :], index[pl.ds(2 * block + 1, 1), :]], axis=1
        )
        onehot = jnp.where(iota((512, 256), 0) == (here & 511), 1.0, 0.0).astype(BF16)
        found = dot(table[...], onehot)
        bank = here >> 9
        value = jnp.zeros((64, 256), F32)
        for hi in range(8):
            high = found[144 * hi : 144 * hi + 64]
            mid = found[144 * hi + 64 : 144 * hi + 128]
            low = found[144 * hi + 128 : 144 * hi + 144]
            mid = jnp.concatenate([mid[:16] + low, mid[16:]], axis=0)
            value = jnp.where(bank == hi, high + mid, value)
        raw_ref[pl.ds(2 * block, 64, stride=32), :] = value[:, :128]
        raw_ref[pl.ds(2 * block + 1, 64, stride=32), :] = value[:, 128:]
        return carry

    lax.fori_loop(0, 16, pick, 0)

    def shape(block, carry):
        camera = camera_block(camera_ref, chosen_ref, block)
        start = pl.multiple_of(block * 8, 8)
        raw = [raw_ref[pl.ds(32 * p + start, 8), :] for p in range(59)]
        for feat, value in enumerate(sent_features(raw, camera)):
            feats[pl.ds(32 * feat + start, 8), :] = value
        return carry

    lax.fori_loop(0, 4, shape, 0)
    for half in range(2):
        lanes = slice(64 * half, 64 * half + 64)
        for pair in range(5):
            left = feats[64 * pair : 64 * pair + 32, lanes]
            if pair < 4:
                right = feats[64 * pair + 32 : 64 * pair + 64, lanes]
            else:
                right = jnp.zeros((32, 64), F32)
            out_ref[pl.ds(160 * half + pair, 32, stride=5), :] = jnp.concatenate(
                [left, right], axis=1
            )


def back_kernel(
    camera_ref, chosen_ref, send_ref, raw_ref, back_ref, first_ref, second_ref,
    index, feats, grads, spread, onehot,
):
    row_index(send_ref, index)
    for pair in range(5):
        near = back_ref[pl.ds(pair, 32, stride=5), :]
        far = back_ref[pl.ds(160 + pair, 32, stride=5), :]
        feats[64 * pair : 64 * pair + 32, :] = jnp.concatenate([near[:, :64], far[:, :64]], axis=1)
        feats[64 * pair + 32 : 64 * pair + 64, :] = jnp.concatenate(
            [near[:, 64:], far[:, 64:]], axis=1
        )
    grads[59 * 32 :, :] = jnp.zeros((5 * 32, 128), F32)

    def pull_back(block, carry):
        camera = camera_block(camera_ref, chosen_ref, block)
        start = pl.multiple_of(block * 8, 8)
        raw = [raw_ref[pl.ds(32 * p + start, 8), :] for p in range(59)]
        _, pull = jax.vjp(lambda rows: sent_features(rows, camera), raw)
        (found,) = pull([feats[pl.ds(32 * feat + start, 8), :] for feat in range(9)])
        for p in range(59):
            grads[pl.ds(32 * p + start, 8), :] = found[p]
        return carry

    lax.fori_loop(0, 4, pull_back, 0)

    def lay(block, carry):
        here = index[pl.ds(block, 1), :]
        lanes = pl.ds(pl.multiple_of(block * 128, 128), 128)
        onehot[:, lanes] = jnp.where(iota((512, 128), 0) == (here & 511), 1.0, 0.0).astype(BF16)
        bank = here >> 9
        high, mid = split2(grads[pl.ds(block, 64, stride=32), :])
        both = jnp.concatenate([high.astype(F32), mid.astype(F32)], axis=0)
        for hi in range(8):
            spread[128 * hi : 128 * hi + 128, lanes] = jnp.where(bank == hi, both, 0.0).astype(BF16)
        return carry

    lax.fori_loop(0, 32, lay, 0)
    for hi in range(8):
        total = dot(spread[128 * hi : 128 * hi + 128, :], onehot[...], NT)
        total = total[:64] + total[64:]
        first_ref[:, 512 * hi : 512 * hi + 512] = total[:32]
        second_ref[:, 512 * hi : 512 * hi + 512] = total[32:]


def whole(space):
    return pl.BlockSpec(memory_space=space)


LIMIT = pltpu.CompilerParams(vmem_limit_bytes=56 * 1024 * 1024)


def send_rows(cameras, chosen, send, params):
    return pl.pallas_call(
        send_kernel,
        out_shape=(
            jax.ShapeDtypeStruct((320, 128), F32),
            jax.ShapeDtypeStruct((2048, 128), F32),
        ),
        in_specs=[whole(pltpu.SMEM), whole(pltpu.SMEM), whole(pltpu.VMEM), whole(pltpu.VMEM)],
        out_specs=(whole(pltpu.VMEM), whole(pltpu.VMEM)),
        scratch_shapes=[
            pltpu.VMEM((8 * 144, 512), BF16),
            pltpu.VMEM((32, 128), I32),
            pltpu.VMEM((9 * 32, 128), F32),
        ],
        compiler_params=LIMIT,
        name="send_rows",
    )(cameras, chosen, send, params)


def pull_rows(cameras, chosen, send, raw, back):
    return pl.pallas_call(
        back_kernel,
        out_shape=(
            jax.ShapeDtypeStruct((32, 4096), F32),
            jax.ShapeDtypeStruct((32, 4096), F32),
        ),
        in_specs=[
            whole(pltpu.SMEM), whole(pltpu.SMEM), whole(pltpu.VMEM), whole(pltpu.VMEM),
            whole(pltpu.VMEM),
        ],
        out_specs=(whole(pltpu.VMEM), whole(pltpu.VMEM)),
        scratch_shapes=[
            pltpu.VMEM((32, 128), I32),
            pltpu.VMEM((10 * 32, 128), F32),
            pltpu.VMEM((2048, 128), F32),
            pltpu.VMEM((1024, 4096), BF16),
            pltpu.VMEM((512, 4096), BF16),
        ],
        compiler_params=LIMIT,
        name="pull_rows",
    )(cameras, chosen, send, raw, back)


def adam_update(params, adam_m, adam_v, gradient):
    rates = jnp.asarray(learn_rates, jnp.float32)[:, None]
    new_m = 0.9 * adam_m + 0.1 * gradient
    new_v = 0.999 * adam_v + 0.001 * gradient * gradient
    new_params = params - rates * (new_m / bias_first) / (jnp.sqrt(new_v / bias_second) + 1e-08)
    return (new_params, new_m, new_v)


def on_device(
    params, adam_m, adam_v, cameras, device_camera, send_index, slot_rows, tile_ids, target
):
    outgoing, raw = send_rows(cameras, device_camera, send_index[0, 0], params)
    incoming = lax.all_to_all(outgoing.reshape(64, 1, 640), "gs", 0, 0, tiled=True)
    colours, back = render(
        incoming.reshape(320, 128), slot_rows[0, 0], tile_ids[0], target[0, 0].transpose(1, 0, 2)
    )
    returned = lax.all_to_all(back.reshape(64, 1, 640), "gs", 0, 0, tiled=True)
    first, second = pull_rows(
        cameras, device_camera, send_index[0, 0], raw, returned.reshape(320, 128)
    )
    first, second = total_over_images(first, second)
    total = jnp.concatenate([first, second], axis=0)[:59]
    new_params, new_m, new_v = adam_update(params, adam_m, adam_v, total)
    return (new_params, new_m, new_v, colours.transpose(1, 0, 2)[None, None])


def total_over_images(first, second):
    near = [(i, i ^ 1) for i in range(4)]
    far = [(i, 3 - i) for i in range(4)]
    first, second = (
        first + lax.ppermute(first, "img", near),
        second + lax.ppermute(second, "img", far),
    )
    return first + lax.ppermute(first, "img", far), second + lax.ppermute(second, "img", near)


def solution(mesh):
    return jax.shard_map(
        on_device,
        mesh=mesh,
        in_specs=(
            P(None, "gs"),
            P(None, "gs"),
            P(None, "gs"),
            P(),
            P("img", None),
            P("img", "gs", None, None),
            P("img", "gs", None, None),
            P("img", "gs", None),
            P("img", "gs", None, None, None),
        ),
        out_specs=(P(None, "gs"), P(None, "gs"), P(None, "gs"), P("img", "gs", None, None, None)),
        check_vma=False,
    )
```

```python
import jax
import jax.numpy as jnp
import numpy as np
from jax import lax
from jax.experimental import pallas as pl
from jax.experimental.pallas import tpu as pltpu
from jax.sharding import PartitionSpec as P

TILE = 16
IMG_TILES = 16


sh_zero = 0.28209479177387814
sh_one = 0.4886025119029199
sh_two = (
    1.0925484305920792,
    -1.0925484305920792,
    0.31539156525252005,
    -1.0925484305920792,
    0.5462742152960396,
)
sh_three = (
    -0.5900435899266435,
    2.890611442640554,
    -0.4570457994644658,
    0.3731763325901154,
    -0.4570457994644658,
    1.445305721320277,
    -0.5900435899266435,
)
learn_rates = np.array(
    [0.00016] * 3 + [0.005] * 3 + [0.001] * 4 + [0.05] + [0.0025] * 3 + [0.000125] * 45
)
LN2 = float(np.log(2.0))
LOG2_E = 1.0 / LN2
LOG_TOP = float(np.log2(0.99))
bias_first = 1.0 - 0.9**10
bias_second = 1.0 - 0.999**10


def sh_basis(dir_x, dir_y, dir_z):
    square_x = dir_x * dir_x
    square_y = dir_y * dir_y
    square_z = dir_z * dir_z
    return [
        sh_zero * jnp.ones_like(dir_x),
        -sh_one * dir_y,
        sh_one * dir_z,
        -sh_one * dir_x,
        sh_two[0] * dir_x * dir_y,
        sh_two[1] * dir_y * dir_z,
        sh_two[2] * (2.0 * square_z - square_x - square_y),
        sh_two[3] * dir_x * dir_z,
        sh_two[4] * (square_x - square_y),
        sh_three[0] * dir_y * (3.0 * square_x - square_y),
        sh_three[1] * dir_x * dir_y * dir_z,
        sh_three[2] * dir_y * (4.0 * square_z - square_x - square_y),
        sh_three[3] * dir_z * (2.0 * square_z - 3.0 * square_x - 3.0 * square_y),
        sh_three[4] * dir_x * (4.0 * square_z - square_x - square_y),
        sh_three[5] * dir_z * (square_x - square_y),
        sh_three[6] * dir_x * (square_x - 3.0 * square_y),
    ]


def sent_features(raw, camera):
    world = [raw[0], raw[1], raw[2]]
    scales = [jnp.exp(raw[3]), jnp.exp(raw[4]), jnp.exp(raw[5])]
    quat_sq = jnp.maximum(
        raw[6] * raw[6] + raw[7] * raw[7] + raw[8] * raw[8] + raw[9] * raw[9], 0.25
    )
    inverse = lax.rsqrt(quat_sq)
    quat_w, quat_x, quat_y, quat_z = (
        raw[6] * inverse,
        raw[7] * inverse,
        raw[8] * inverse,
        raw[9] * inverse,
    )
    rotation = [
        [
            1.0 - 2.0 * (quat_y * quat_y + quat_z * quat_z),
            2.0 * (quat_x * quat_y - quat_w * quat_z),
            2.0 * (quat_x * quat_z + quat_w * quat_y),
        ],
        [
            2.0 * (quat_x * quat_y + quat_w * quat_z),
            1.0 - 2.0 * (quat_x * quat_x + quat_z * quat_z),
            2.0 * (quat_y * quat_z - quat_w * quat_x),
        ],
        [
            2.0 * (quat_x * quat_z - quat_w * quat_y),
            2.0 * (quat_y * quat_z + quat_w * quat_x),
            1.0 - 2.0 * (quat_x * quat_x + quat_y * quat_y),
        ],
    ]
    spread = [
        [rotation[first][second] * scales[second] for second in range(3)] for first in range(3)
    ]
    turn = [[camera[3 * first + second] for second in range(3)] for first in range(3)]
    viewed = [
        turn[first][0] * world[0]
        + turn[first][1] * world[1]
        + turn[first][2] * world[2]
        + camera[9 + first]
        for first in range(3)
    ]
    inv_depth = 1.0 / viewed[2]
    focal = camera[15]
    jacobian = [
        [focal * inv_depth, 0.0 * inv_depth, -focal * viewed[0] * inv_depth * inv_depth],
        [0.0 * inv_depth, focal * inv_depth, -focal * viewed[1] * inv_depth * inv_depth],
    ]
    screen = [
        [
            sum((jacobian[first][inner] * turn[inner][second] for inner in range(3)))
            for second in range(3)
        ]
        for first in range(2)
    ]
    mapped = [
        [
            sum((screen[first][inner] * spread[inner][second] for inner in range(3)))
            for second in range(3)
        ]
        for first in range(2)
    ]
    cov_xx = sum((mapped[0][inner] * mapped[0][inner] for inner in range(3))) + 0.3
    cov_xy = sum((mapped[0][inner] * mapped[1][inner] for inner in range(3)))
    cov_yy = sum((mapped[1][inner] * mapped[1][inner] for inner in range(3))) + 0.3
    determinant = cov_xx * cov_yy - cov_xy * cov_xy
    half_width = 0.5 * IMG_TILES * TILE
    ray = [world[first] - camera[12 + first] for first in range(3)]
    ray_scale = lax.rsqrt(ray[0] * ray[0] + ray[1] * ray[1] + ray[2] * ray[2])
    basis = sh_basis(ray[0] * ray_scale, ray[1] * ray_scale, ray[2] * ray_scale)
    colours = [
        jnp.maximum(
            sum((basis[term] * raw[11 + 3 * term + channel] for term in range(16))) + 0.5, 0.0
        )
        for channel in range(3)
    ]
    inverse_det = 1.0 / determinant
    log_opacity = LOG_TOP - jnp.log(1.0 + jnp.exp(-raw[10])) * LOG2_E
    return [
        focal * viewed[0] * inv_depth + half_width,
        focal * viewed[1] * inv_depth + half_width,
        (-0.5 * LOG2_E) * cov_yy * inverse_det,
        LOG2_E * cov_xy * inverse_det,
        (-0.5 * LOG2_E) * cov_xx * inverse_det,
        log_opacity,
        colours[0],
        colours[1],
        colours[2],
    ]


F32, BF16, I32 = jnp.float32, jnp.bfloat16, jnp.int32
NN = (((1,), (0,)), ((), ()))
NT = (((1,), (1,)), ((), ()))


def dot(left, right, dims=NN):
    return lax.dot_general(left, right, dims, preferred_element_type=F32)


def split2(value):
    high = value.astype(BF16)
    return high, (value - high.astype(F32)).astype(BF16)


def split3(value):
    high = value.astype(BF16)
    rest = value - high.astype(F32)
    mid = rest.astype(BF16)
    return high, mid, (rest - mid.astype(F32)).astype(BF16)


def iota(shape, dim):
    return lax.broadcasted_iota(I32, shape, dim)


def wide(tinted, at, ch):
    value = tinted[at, 128 * ch : 128 * ch + 128]
    return jnp.concatenate([value, value], axis=1)


def render_kernel(
    tid_ref, recv_ref, slots_ref, target_ref, colour_ref, out_ref,
    table, onehot, coef, power_w, turned, alpha, weight, weight_h, weight_l, pixel_w,
    spread, total, tint_w, tinted,
):
    groups, _, rows = slots_ref.shape
    many = target_ref.shape[1] // groups
    tints = 3 * many
    edge = 16 + 2 * tints
    chunks = rows // 256
    depth = coef.shape[0]
    for feat in range(9):
        side = slice(64 * (feat % 2), 64 * (feat % 2) + 64)
        block = jnp.concatenate(
            [recv_ref[pl.ds(80 * j + feat // 2, 16, stride=5), :][:, side] for j in range(4)],
            axis=1,
        )
        for part, piece in enumerate(split3(block)):
            table[pl.ds((part * 9 + feat) * 16, 16), :] = piece
    total[...] = jnp.zeros_like(total)
    coef[...] = jnp.zeros_like(coef)
    def pick(kind, u, v):
        out = jnp.where(kind == 0, 1.0, 0.0)
        out = jnp.where(kind == 1, u, out)
        out = jnp.where(kind == 2, v, out)
        out = jnp.where(kind == 3, u * u, out)
        out = jnp.where(kind == 4, u * v, out)
        return jnp.where(kind == 5, v * v, out)
    pix = iota((256, 128), 0)
    mono = pick(
        iota((256, 128), 1), (pix & 15).astype(F32) - 7.5, (pix >> 4).astype(F32) - 7.5
    ).astype(BF16)
    pixel_w[:256, :] = mono
    pixel_w[256:512, :] = mono
    row = iota((depth, 256), 0)
    pix = iota((depth, 256), 1)
    kind = jnp.where(row >= 12, row - 12, jnp.where(row >= 6, row - 6, row))
    power_w[...] = jnp.where(
        row < 18,
        pick(kind, (pix & 15).astype(F32) - 7.5, (pix >> 4).astype(F32) - 7.5),
        0.0,
    ).astype(BF16)

    row = iota((depth, 384), 0)
    first_row = 18 + 3 * (iota((depth, 384), 1) >> 7)
    tint_w[...] = jnp.where((row >= first_row) & (row < first_row + 3), 1.0, 0.0).astype(BF16)

    lane_tile = iota((1, rows), 1) & (many - 1)
    own = iota((many, rows), 0) == lane_tile
    hi_row = iota((16, rows), 0)

    def group(step, carry):
        index = slots_ref[step]
        live = index >= 0
        low = ((index >> 10) << 6) | (index & 63)
        high = jnp.where(live, (index >> 6) & 15, -1)
        onehot[...] = jnp.where(iota((256, rows), 0) == low, 1.0, 0.0).astype(BF16)
        mask = hi_row == high
        raw = dot(table[...], onehot[...])
        feats = []
        for feat in range(9):
            part = (
                raw[288 + 16 * feat : 304 + 16 * feat] + raw[144 + 16 * feat : 160 + 16 * feat]
            ) + raw[16 * feat : 16 * feat + 16]
            feats.append(jnp.sum(jnp.where(mask, part, 0.0), axis=0, keepdims=True))
        mean_x, mean_y, con_a, con_b, con_c, log_op = feats[:6]
        centre_x = jnp.zeros((1, rows), F32)
        centre_y = jnp.zeros((1, rows), F32)
        for t in range(many):
            tid = tid_ref[0, step * many + t]
            centre_x = jnp.where(lane_tile == t, ((tid & 15) * 16 + 8).astype(F32), centre_x)
            centre_y = jnp.where(lane_tile == t, ((tid >> 4) * 16 + 8).astype(F32), centre_y)
        far_x = centre_x - mean_x
        far_y = centre_y - mean_y
        ax = con_a * far_x
        bx = con_b * far_x
        by = con_b * far_y
        cy = con_c * far_y
        constant = far_x * (ax + by) + far_y * cy + log_op
        constant = jnp.where(live, constant, -1e30)
        for m, value in enumerate(
            (constant, 2.0 * ax + by, bx + 2.0 * cy, con_a, con_b, con_c)
        ):
            for part, piece in enumerate(split3(value)):
                coef[pl.ds(part * 6 + m, 1), :] = piece.astype(F32)
        for ch in range(3):
            for part, piece in enumerate(split3(feats[6 + ch])):
                coef[pl.ds(18 + 3 * ch + part, 1), :] = piece.astype(F32)
        turned[...] = jnp.transpose(coef[...]).astype(BF16)

        passed = jnp.ones((many, 256), F32)
        shown = [jnp.zeros((many, 256), F32)] * 3
        for chunk in range(chunks):
            part = slice(256 * chunk, 256 * chunk + 256)
            alphas = jnp.exp2(dot(turned[part, :], power_w[...]))
            tinted[part, :] = dot(turned[part, :], tint_w[...])
            alpha[part, :] = alphas
            out = []
            for k in range(0, 256, many):
                w = passed * alphas[k : k + many]
                passed = passed - w
                at = slice(256 * chunk + k, 256 * chunk + k + many)
                shown = [value + w * wide(tinted, at, ch) for ch, value in enumerate(shown)]
                out.append(w)
            out = jnp.concatenate(out, axis=0)
            weight[part, :] = out
            w_h, w_l = split2(out)
            weight_h[part, :] = w_h
            weight_l[part, :] = w_l
        diffs = []
        for ch in range(3):
            where = pl.ds(pl.multiple_of(step * many, many), many)
            colour_ref[ch, where, :] = shown[ch]
            diffs.append(shown[ch] - target_ref[ch, where, :])
        d_high = [value.astype(BF16).astype(F32) for value in diffs]
        d_mid = [value - high for value, high in zip(diffs, d_high)]
        front = jnp.zeros((16, 256), F32)
        back = jnp.zeros((128 - edge, 256), F32)
        pixel_w[512:768, :] = jnp.transpose(
            jnp.concatenate([front] + d_high + d_mid + [back], axis=0)
        ).astype(BF16)
        pixel_w[768:, :] = jnp.transpose(
            jnp.concatenate([front] + d_high + [jnp.zeros((112 - tints, 256), F32)], axis=0)
        ).astype(BF16)

        behind = jnp.zeros((many, 256), F32)
        sums = [None] * chunks
        for chunk in range(chunks - 1, -1, -1):
            part = slice(256 * chunk, 256 * chunk + 256)
            alphas = alpha[part, :]
            weights = weight[part, :]
            out = []
            for k in range(256 - many, -1, -many):
                at = slice(256 * chunk + k, 256 * chunk + k + many)
                pulls = (
                    diffs[0] * wide(tinted, at, 0) + diffs[1] * wide(tinted, at, 1)
                ) + diffs[2] * wide(tinted, at, 2)
                gap = pulls - behind
                out.append(weights[k : k + many] * gap)
                behind = behind + alphas[k : k + many] * gap
            d_h, d_l = split2(jnp.concatenate(out[::-1], axis=0))
            both = jnp.concatenate([d_h, d_l, weight_h[part, :], weight_l[part, :]], axis=1)
            sums[chunk] = jnp.transpose(dot(both, pixel_w[...]))
        sums = jnp.concatenate(sums, axis=1)
        moments = sums[:16]
        tint = sums[16 : 16 + tints] + sums[16 + tints : edge]
        s_0, s_u, s_v, s_uu, s_uv, s_vv = [LN2 * moments[m : m + 1] for m in range(6)]
        sum_x = far_x * s_0 + s_u
        sum_y = far_y * s_0 + s_v
        grads = [
            -(2.0 * con_a * sum_x + con_b * sum_y),
            -(con_b * sum_x + 2.0 * con_c * sum_y),
            far_x * (sum_x + s_u) + s_uu,
            far_x * sum_y + far_y * s_u + s_uv,
            far_y * (sum_y + s_v) + s_vv,
            s_0,
        ] + [
            jnp.sum(
                jnp.where(own, tint[many * ch : many * ch + many], 0.0), axis=0, keepdims=True
            )
            for ch in range(3)
        ]
        for feat in range(9):
            for part, piece in enumerate(split2(grads[feat])):
                spread[pl.ds((part * 9 + feat) * 16, 16), :] = jnp.where(
                    mask, piece.astype(F32), 0.0
                ).astype(BF16)
        total[...] += dot(spread[...], onehot[...], NT)
        return carry

    lax.fori_loop(0, groups, group, 0)
    grids = []
    for feat in range(9):
        grids.append(total[16 * feat + 144 : 16 * feat + 160] + total[16 * feat : 16 * feat + 16])
    grids.append(jnp.zeros((16, 256), F32))
    for pair in range(5):
        for j in range(4):
            lanes = slice(64 * j, 64 * j + 64)
            out_ref[pl.ds(80 * j + pair, 16, stride=5), :] = jnp.concatenate(
                [grids[2 * pair][:, lanes], grids[2 * pair + 1][:, lanes]], axis=1
            )


def render(recv, slot_rows, tile_ids, target, many=16):
    tiles, slots = slot_rows.shape
    groups = tiles // many
    rows = slots * many
    depth = 32
    ordered = slot_rows.reshape(groups, many, slots).transpose(0, 2, 1).reshape(groups, 1, rows)
    return pl.pallas_call(
        render_kernel,
        out_shape=(
            jax.ShapeDtypeStruct((3, tiles, 256), F32),
            jax.ShapeDtypeStruct((320, 128), F32),
        ),
        in_specs=[whole(pltpu.SMEM)] + [whole(pltpu.VMEM)] * 3,
        out_specs=(whole(pltpu.VMEM), whole(pltpu.VMEM)),
        scratch_shapes=[
            pltpu.VMEM((432, 256), BF16),
            pltpu.VMEM((256, rows), BF16),
            pltpu.VMEM((depth, rows), F32),
            pltpu.VMEM((depth, 256), BF16),
            pltpu.VMEM((rows, depth), BF16),
            pltpu.VMEM((rows, 256), F32),
            pltpu.VMEM((rows, 256), F32),
            pltpu.VMEM((rows, 256), BF16),
            pltpu.VMEM((rows, 256), BF16),
            pltpu.VMEM((1024, 128), BF16),
            pltpu.VMEM((288, rows), BF16),
            pltpu.VMEM((288, 256), F32),
            pltpu.VMEM((depth, 384), BF16),
            pltpu.VMEM((rows, 384), F32),
        ],
        compiler_params=LIMIT,
        name="render",
    )(tile_ids, recv, ordered, target)


def camera_block(camera_ref, chosen_ref, block):
    lane = iota((8, 128), 1)
    sub = iota((8, 128), 0)
    which = jnp.zeros((8, 128), I32)
    for k in range(8):
        near = chosen_ref[0, block * 8 + k]
        far = chosen_ref[0, 32 + block * 8 + k]
        which = jnp.where(sub == k, jnp.where(lane < 64, near, far), which)
    values = [jnp.zeros((8, 128), F32) for _ in range(16)]
    for cam in range(16):
        here = which == cam
        values = [
            jnp.where(here, camera_ref[k, cam], value) for k, value in enumerate(values)
        ]
    return values


def row_index(send_ref, index):
    index[...] = jnp.concatenate([send_ref[:32, :], send_ref[32:, :]], axis=1)


def send_kernel(camera_ref, chosen_ref, send_ref, params_ref, out_ref, raw_ref, table, index, feats):
    row_index(send_ref, index)
    for hi in range(8):
        piece = params_ref[:, 512 * hi : 512 * hi + 512]
        piece = jnp.concatenate([piece, jnp.zeros((5, 512), F32)], axis=0)
        high, mid, low = split3(piece)
        table[144 * hi : 144 * hi + 64, :] = high
        table[144 * hi + 64 : 144 * hi + 128, :] = mid
        table[144 * hi + 128 : 144 * hi + 144, :] = low[:16]

    def pick(block):
        here = jnp.concatenate(
            [index[pl.ds(2 * block, 1), :], index[pl.ds(2 * block + 1, 1), :]], axis=1
        )
        onehot = jnp.where(iota((512, 256), 0) == (here & 511), 1.0, 0.0).astype(BF16)
        found = dot(table[...], onehot)
        bank = here >> 9
        value = jnp.zeros((64, 256), F32)
        for hi in range(8):
            high = found[144 * hi : 144 * hi + 64]
            mid = found[144 * hi + 64 : 144 * hi + 128]
            low = found[144 * hi + 128 : 144 * hi + 144]
            mid = jnp.concatenate([mid[:16] + low, mid[16:]], axis=0)
            value = jnp.where(bank == hi, high + mid, value)
        raw_ref[pl.ds(2 * block, 64, stride=32), :] = value[:, :128]
        raw_ref[pl.ds(2 * block + 1, 64, stride=32), :] = value[:, 128:]

    for block in range(16):
        pick(block)

    def shape(block, carry):
        camera = camera_block(camera_ref, chosen_ref, block)
        start = pl.multiple_of(block * 8, 8)
        raw = [raw_ref[pl.ds(32 * p + start, 8), :] for p in range(59)]
        for feat, value in enumerate(sent_features(raw, camera)):
            feats[pl.ds(32 * feat + start, 8), :] = value
        return carry

    lax.fori_loop(0, 4, shape, 0)
    for half in range(2):
        lanes = slice(64 * half, 64 * half + 64)
        for pair in range(5):
            left = feats[64 * pair : 64 * pair + 32, lanes]
            if pair < 4:
                right = feats[64 * pair + 32 : 64 * pair + 64, lanes]
            else:
                right = jnp.zeros((32, 64), F32)
            out_ref[pl.ds(160 * half + pair, 32, stride=5), :] = jnp.concatenate(
                [left, right], axis=1
            )


def back_kernel(
    camera_ref, chosen_ref, send_ref, raw_ref, back_ref, first_ref, second_ref,
    index, feats, grads, spread, onehot,
):
    row_index(send_ref, index)
    for pair in range(5):
        near = back_ref[pl.ds(pair, 32, stride=5), :]
        far = back_ref[pl.ds(160 + pair, 32, stride=5), :]
        feats[64 * pair : 64 * pair + 32, :] = jnp.concatenate([near[:, :64], far[:, :64]], axis=1)
        feats[64 * pair + 32 : 64 * pair + 64, :] = jnp.concatenate(
            [near[:, 64:], far[:, 64:]], axis=1
        )
    grads[59 * 32 :, :] = jnp.zeros((5 * 32, 128), F32)

    def pull_back(block, carry):
        camera = camera_block(camera_ref, chosen_ref, block)
        start = pl.multiple_of(block * 8, 8)
        raw = [raw_ref[pl.ds(32 * p + start, 8), :] for p in range(59)]
        _, pull = jax.vjp(lambda rows: sent_features(rows, camera), raw)
        (found,) = pull([feats[pl.ds(32 * feat + start, 8), :] for feat in range(9)])
        for p in range(59):
            grads[pl.ds(32 * p + start, 8), :] = found[p]
        return carry

    lax.fori_loop(0, 4, pull_back, 0)

    def lay(block):
        here = index[pl.ds(block, 1), :]
        lanes = slice(128 * block, 128 * block + 128)
        onehot[:, lanes] = jnp.where(iota((512, 128), 0) == (here & 511), 1.0, 0.0).astype(BF16)
        bank = here >> 9
        high, mid = split2(grads[pl.ds(block, 64, stride=32), :])
        both = jnp.concatenate([high, mid], axis=0)
        for hi in range(8):
            chosen = jnp.where(bank == hi, 1.0, 0.0).astype(BF16)
            spread[128 * hi : 128 * hi + 128, lanes] = both * chosen

    everything = jnp.zeros((1024, 512), F32)
    for part in range(4):
        for block in range(8 * part, 8 * part + 8):
            lay(block)
        lanes = slice(1024 * part, 1024 * part + 1024)
        everything = everything + dot(spread[:, lanes], onehot[:, lanes], NT)
    for hi in range(8):
        total = everything[128 * hi : 128 * hi + 64] + everything[128 * hi + 64 : 128 * hi + 128]
        first_ref[:, 512 * hi : 512 * hi + 512] = total[:32]
        second_ref[:, 512 * hi : 512 * hi + 512] = total[32:]


def whole(space):
    return pl.BlockSpec(memory_space=space)


LIMIT = pltpu.CompilerParams(vmem_limit_bytes=56 * 1024 * 1024)


def send_rows(cameras, chosen, send, params):
    return pl.pallas_call(
        send_kernel,
        out_shape=(
            jax.ShapeDtypeStruct((320, 128), F32),
            jax.ShapeDtypeStruct((2048, 128), F32),
        ),
        in_specs=[whole(pltpu.SMEM), whole(pltpu.SMEM), whole(pltpu.VMEM), whole(pltpu.VMEM)],
        out_specs=(whole(pltpu.VMEM), whole(pltpu.VMEM)),
        scratch_shapes=[
            pltpu.VMEM((8 * 144, 512), BF16),
            pltpu.VMEM((32, 128), I32),
            pltpu.VMEM((9 * 32, 128), F32),
        ],
        compiler_params=LIMIT,
        name="send_rows",
    )(cameras, chosen, send, params)


def pull_rows(cameras, chosen, send, raw, back):
    return pl.pallas_call(
        back_kernel,
        out_shape=(
            jax.ShapeDtypeStruct((32, 4096), F32),
            jax.ShapeDtypeStruct((32, 4096), F32),
        ),
        in_specs=[
            whole(pltpu.SMEM), whole(pltpu.SMEM), whole(pltpu.VMEM), whole(pltpu.VMEM),
            whole(pltpu.VMEM),
        ],
        out_specs=(whole(pltpu.VMEM), whole(pltpu.VMEM)),
        scratch_shapes=[
            pltpu.VMEM((32, 128), I32),
            pltpu.VMEM((10 * 32, 128), F32),
            pltpu.VMEM((2048, 128), F32),
            pltpu.VMEM((1024, 4096), BF16),
            pltpu.VMEM((512, 4096), BF16),
        ],
        compiler_params=LIMIT,
        name="pull_rows",
    )(cameras, chosen, send, raw, back)


def adam_update(params, adam_m, adam_v, gradient):
    rates = jnp.asarray(learn_rates, jnp.float32)[:, None]
    new_m = 0.9 * adam_m + 0.1 * gradient
    new_v = 0.999 * adam_v + 0.001 * gradient * gradient
    new_params = params - rates * (new_m / bias_first) / (jnp.sqrt(new_v / bias_second) + 1e-08)
    return (new_params, new_m, new_v)


def on_device(
    params, adam_m, adam_v, cameras, device_camera, send_index, slot_rows, tile_ids, target
):
    outgoing, raw = send_rows(cameras, device_camera, send_index[0, 0], params)
    incoming = lax.all_to_all(outgoing.reshape(64, 1, 640), "gs", 0, 0, tiled=True)
    colours, back = render(
        incoming.reshape(320, 128), slot_rows[0, 0], tile_ids[0], target[0, 0].transpose(1, 0, 2)
    )
    returned = lax.all_to_all(back.reshape(64, 1, 640), "gs", 0, 0, tiled=True)
    first, second = pull_rows(
        cameras, device_camera, send_index[0, 0], raw, returned.reshape(320, 128)
    )
    first, second = total_over_images(first, second)
    total = jnp.concatenate([first, second], axis=0)[:59]
    new_params, new_m, new_v = adam_update(params, adam_m, adam_v, total)
    return (new_params, new_m, new_v, colours.transpose(1, 0, 2)[None, None])


def total_over_images(first, second):
    near = [(i, i ^ 1) for i in range(4)]
    far = [(i, 3 - i) for i in range(4)]
    first, second = (
        first + lax.ppermute(first, "img", near),
        second + lax.ppermute(second, "img", far),
    )
    return first + lax.ppermute(first, "img", far), second + lax.ppermute(second, "img", near)


def solution(mesh):
    return jax.shard_map(
        on_device,
        mesh=mesh,
        in_specs=(
            P(None, "gs"),
            P(None, "gs"),
            P(None, "gs"),
            P(),
            P("img", None),
            P("img", "gs", None, None),
            P("img", "gs", None, None),
            P("img", "gs", None),
            P("img", "gs", None, None, None),
        ),
        out_specs=(P(None, "gs"), P(None, "gs"), P(None, "gs"), P("img", "gs", None, None, None)),
        check_vma=False,
    )
```

```python
import jax
import jax.numpy as jnp
import numpy as np
from jax import lax
from jax.experimental import pallas as pl
from jax.experimental.pallas import tpu as pltpu
from jax.sharding import PartitionSpec as P

TILE = 16
IMG_TILES = 16


sh_zero = 0.28209479177387814
sh_one = 0.4886025119029199
sh_two = (
    1.0925484305920792,
    -1.0925484305920792,
    0.31539156525252005,
    -1.0925484305920792,
    0.5462742152960396,
)
sh_three = (
    -0.5900435899266435,
    2.890611442640554,
    -0.4570457994644658,
    0.3731763325901154,
    -0.4570457994644658,
    1.445305721320277,
    -0.5900435899266435,
)
learn_rates = np.array(
    [0.00016] * 3 + [0.005] * 3 + [0.001] * 4 + [0.05] + [0.0025] * 3 + [0.000125] * 45
)
LN2 = float(np.log(2.0))
LOG2_E = 1.0 / LN2
LOG_TOP = float(np.log2(0.99))
bias_first = 1.0 - 0.9**10
bias_second = 1.0 - 0.999**10


def sh_basis(dir_x, dir_y, dir_z):
    square_x = dir_x * dir_x
    square_y = dir_y * dir_y
    square_z = dir_z * dir_z
    return [
        sh_zero * jnp.ones_like(dir_x),
        -sh_one * dir_y,
        sh_one * dir_z,
        -sh_one * dir_x,
        sh_two[0] * dir_x * dir_y,
        sh_two[1] * dir_y * dir_z,
        sh_two[2] * (2.0 * square_z - square_x - square_y),
        sh_two[3] * dir_x * dir_z,
        sh_two[4] * (square_x - square_y),
        sh_three[0] * dir_y * (3.0 * square_x - square_y),
        sh_three[1] * dir_x * dir_y * dir_z,
        sh_three[2] * dir_y * (4.0 * square_z - square_x - square_y),
        sh_three[3] * dir_z * (2.0 * square_z - 3.0 * square_x - 3.0 * square_y),
        sh_three[4] * dir_x * (4.0 * square_z - square_x - square_y),
        sh_three[5] * dir_z * (square_x - square_y),
        sh_three[6] * dir_x * (square_x - 3.0 * square_y),
    ]


def direction(raw, camera):
    ray = [raw[first] - camera[12 + first] for first in range(3)]
    ray_scale = lax.rsqrt(ray[0] * ray[0] + ray[1] * ray[1] + ray[2] * ray[2])
    return [ray[0] * ray_scale, ray[1] * ray_scale, ray[2] * ray_scale]


def sent_features(raw, camera):
    world = [raw[0], raw[1], raw[2]]
    scales = [jnp.exp(raw[3]), jnp.exp(raw[4]), jnp.exp(raw[5])]
    quat_sq = jnp.maximum(
        raw[6] * raw[6] + raw[7] * raw[7] + raw[8] * raw[8] + raw[9] * raw[9], 0.25
    )
    inverse = lax.rsqrt(quat_sq)
    quat_w, quat_x, quat_y, quat_z = (
        raw[6] * inverse,
        raw[7] * inverse,
        raw[8] * inverse,
        raw[9] * inverse,
    )
    rotation = [
        [
            1.0 - 2.0 * (quat_y * quat_y + quat_z * quat_z),
            2.0 * (quat_x * quat_y - quat_w * quat_z),
            2.0 * (quat_x * quat_z + quat_w * quat_y),
        ],
        [
            2.0 * (quat_x * quat_y + quat_w * quat_z),
            1.0 - 2.0 * (quat_x * quat_x + quat_z * quat_z),
            2.0 * (quat_y * quat_z - quat_w * quat_x),
        ],
        [
            2.0 * (quat_x * quat_z - quat_w * quat_y),
            2.0 * (quat_y * quat_z + quat_w * quat_x),
            1.0 - 2.0 * (quat_x * quat_x + quat_y * quat_y),
        ],
    ]
    spread = [
        [rotation[first][second] * scales[second] for second in range(3)] for first in range(3)
    ]
    turn = [[camera[3 * first + second] for second in range(3)] for first in range(3)]
    viewed = [
        turn[first][0] * world[0]
        + turn[first][1] * world[1]
        + turn[first][2] * world[2]
        + camera[9 + first]
        for first in range(3)
    ]
    inv_depth = 1.0 / viewed[2]
    focal = camera[15]
    jacobian = [
        [focal * inv_depth, 0.0 * inv_depth, -focal * viewed[0] * inv_depth * inv_depth],
        [0.0 * inv_depth, focal * inv_depth, -focal * viewed[1] * inv_depth * inv_depth],
    ]
    screen = [
        [
            sum((jacobian[first][inner] * turn[inner][second] for inner in range(3)))
            for second in range(3)
        ]
        for first in range(2)
    ]
    mapped = [
        [
            sum((screen[first][inner] * spread[inner][second] for inner in range(3)))
            for second in range(3)
        ]
        for first in range(2)
    ]
    cov_xx = sum((mapped[0][inner] * mapped[0][inner] for inner in range(3))) + 0.3
    cov_xy = sum((mapped[0][inner] * mapped[1][inner] for inner in range(3)))
    cov_yy = sum((mapped[1][inner] * mapped[1][inner] for inner in range(3))) + 0.3
    determinant = cov_xx * cov_yy - cov_xy * cov_xy
    half_width = 0.5 * IMG_TILES * TILE
    basis = sh_basis(*direction(raw, camera))
    colours = [
        jnp.maximum(
            sum((basis[term] * raw[11 + 3 * term + channel] for term in range(16))) + 0.5, 0.0
        )
        for channel in range(3)
    ]
    inverse_det = 1.0 / determinant
    log_opacity = LOG_TOP - jnp.log(1.0 + jnp.exp(-raw[10])) * LOG2_E
    return [
        focal * viewed[0] * inv_depth + half_width,
        focal * viewed[1] * inv_depth + half_width,
        (-0.5 * LOG2_E) * cov_yy * inverse_det,
        LOG2_E * cov_xy * inverse_det,
        (-0.5 * LOG2_E) * cov_xx * inverse_det,
        log_opacity,
        colours[0],
        colours[1],
        colours[2],
    ]


F32, BF16, I32 = jnp.float32, jnp.bfloat16, jnp.int32
NN = (((1,), (0,)), ((), ()))
NT = (((1,), (1,)), ((), ()))


def dot(left, right, dims=NN):
    return lax.dot_general(left, right, dims, preferred_element_type=F32)


def split2(value):
    high = value.astype(BF16)
    return high, (value - high.astype(F32)).astype(BF16)


def split3(value):
    high = value.astype(BF16)
    rest = value - high.astype(F32)
    mid = rest.astype(BF16)
    return high, mid, (rest - mid.astype(F32)).astype(BF16)


def iota(shape, dim):
    return lax.broadcasted_iota(I32, shape, dim)


def wide(tinted, at, ch):
    value = tinted[at, 128 * ch : 128 * ch + 128]
    return jnp.concatenate([value, value], axis=1)


def render_kernel(
    tid_ref, recv_ref, slots_ref, target_ref, colour_ref, out_ref,
    table, power_w, tint_w, total, *by_group,
):
    groups, rows = slots_ref.shape[0], slots_ref.shape[1] * 128
    many = target_ref.shape[1] // groups
    tints = 3 * many
    edge = 16 + 2 * tints
    chunks = rows // 256
    depth = power_w.shape[0]
    for feat in range(9):
        side = slice(64 * (feat % 2), 64 * (feat % 2) + 64)
        block = jnp.concatenate(
            [recv_ref[pl.ds(80 * j + feat // 2, 16, stride=5), :][:, side] for j in range(4)],
            axis=1,
        )
        for part, piece in enumerate(split3(block)):
            table[pl.ds((part * 9 + feat) * 16, 16), :] = piece
    total[...] = jnp.zeros_like(total)
    def pick(kind, u, v):
        out = jnp.where(kind == 0, 1.0, 0.0)
        out = jnp.where(kind == 1, u, out)
        out = jnp.where(kind == 2, v, out)
        out = jnp.where(kind == 3, u * u, out)
        out = jnp.where(kind == 4, u * v, out)
        return jnp.where(kind == 5, v * v, out)
    pix = iota((256, 128), 0)
    mono = pick(
        iota((256, 128), 1), (pix & 15).astype(F32) - 7.5, (pix >> 4).astype(F32) - 7.5
    ).astype(BF16)
    row = iota((depth, 256), 0)
    pix = iota((depth, 256), 1)
    kind = jnp.where(row >= 12, row - 12, jnp.where(row >= 6, row - 6, row))
    power_w[...] = jnp.where(
        row < 18,
        pick(kind, (pix & 15).astype(F32) - 7.5, (pix >> 4).astype(F32) - 7.5),
        0.0,
    ).astype(BF16)

    row = iota((depth, 384), 0)
    first_row = 18 + 3 * (iota((depth, 384), 1) >> 7)
    tint_w[...] = jnp.where((row >= first_row) & (row < first_row + 3), 1.0, 0.0).astype(BF16)

    lane_tile = iota((1, rows), 1) & (many - 1)
    own = iota((many, rows), 0) == lane_tile
    hi_row = iota((16, rows), 0)

    def group(step):
        (
            onehot, coef, turned, alpha, weight, weight_h, weight_l, pixel_w, spread, tinted
        ) = [scratch.at[step] for scratch in by_group]
        coef[...] = jnp.zeros((depth, rows), F32)
        pixel_w[:256, :] = mono
        pixel_w[256:512, :] = mono
        index = jnp.concatenate(
            [slots_ref[step, pl.ds(block, 1), :] for block in range(rows // 128)], axis=1
        )
        live = index >= 0
        low = ((index >> 10) << 6) | (index & 63)
        high = jnp.where(live, (index >> 6) & 15, -1)
        onehot[...] = jnp.where(iota((256, rows), 0) == low, 1.0, 0.0).astype(BF16)
        mask = hi_row == high
        raw = dot(table[...], onehot[...])
        feats = []
        for feat in range(9):
            part = (
                raw[288 + 16 * feat : 304 + 16 * feat] + raw[144 + 16 * feat : 160 + 16 * feat]
            ) + raw[16 * feat : 16 * feat + 16]
            feats.append(jnp.sum(jnp.where(mask, part, 0.0), axis=0, keepdims=True))
        mean_x, mean_y, con_a, con_b, con_c, log_op = feats[:6]
        centre_x = jnp.zeros((1, rows), F32)
        centre_y = jnp.zeros((1, rows), F32)
        for t in range(many):
            tid = tid_ref[0, step * many + t]
            centre_x = jnp.where(lane_tile == t, ((tid & 15) * 16 + 8).astype(F32), centre_x)
            centre_y = jnp.where(lane_tile == t, ((tid >> 4) * 16 + 8).astype(F32), centre_y)
        far_x = centre_x - mean_x
        far_y = centre_y - mean_y
        ax = con_a * far_x
        bx = con_b * far_x
        by = con_b * far_y
        cy = con_c * far_y
        constant = far_x * (ax + by) + far_y * cy + log_op
        constant = jnp.where(live, constant, -1e30)
        for m, value in enumerate(
            (constant, 2.0 * ax + by, bx + 2.0 * cy, con_a, con_b, con_c)
        ):
            for part, piece in enumerate(split3(value)):
                coef[pl.ds(part * 6 + m, 1), :] = piece.astype(F32)
        for ch in range(3):
            for part, piece in enumerate(split3(feats[6 + ch])):
                coef[pl.ds(18 + 3 * ch + part, 1), :] = piece.astype(F32)
        turned[...] = jnp.transpose(coef[...]).astype(BF16)

        passed = jnp.ones((many, 256), F32)
        shown = [jnp.zeros((many, 256), F32)] * 3
        for chunk in range(chunks):
            part = slice(256 * chunk, 256 * chunk + 256)
            alphas = jnp.exp2(dot(turned[part, :], power_w[...]))
            tinted[part, :] = dot(turned[part, :], tint_w[...])
            alpha[part, :] = alphas
            out = []
            for k in range(0, 256, many):
                w = passed * alphas[k : k + many]
                passed = passed - w
                at = slice(256 * chunk + k, 256 * chunk + k + many)
                shown = [value + w * wide(tinted, at, ch) for ch, value in enumerate(shown)]
                out.append(w)
            out = jnp.concatenate(out, axis=0)
            weight[part, :] = out
            w_h, w_l = split2(out)
            weight_h[part, :] = w_h
            weight_l[part, :] = w_l
        diffs = []
        for ch in range(3):
            where = slice(step * many, step * many + many)
            colour_ref[ch, where, :] = shown[ch]
            diffs.append(shown[ch] - target_ref[ch, where, :])
        d_high = [value.astype(BF16).astype(F32) for value in diffs]
        d_mid = [value - high for value, high in zip(diffs, d_high)]
        front = jnp.zeros((16, 256), F32)
        back = jnp.zeros((128 - edge, 256), F32)
        pixel_w[512:768, :] = jnp.transpose(
            jnp.concatenate([front] + d_high + d_mid + [back], axis=0)
        ).astype(BF16)
        pixel_w[768:, :] = jnp.transpose(
            jnp.concatenate([front] + d_high + [jnp.zeros((112 - tints, 256), F32)], axis=0)
        ).astype(BF16)

        behind = jnp.zeros((many, 256), F32)
        sums = [None] * chunks
        for chunk in range(chunks - 1, -1, -1):
            part = slice(256 * chunk, 256 * chunk + 256)
            alphas = alpha[part, :]
            weights = weight[part, :]
            out = []
            for k in range(256 - many, -1, -many):
                at = slice(256 * chunk + k, 256 * chunk + k + many)
                pulls = (
                    diffs[0] * wide(tinted, at, 0) + diffs[1] * wide(tinted, at, 1)
                ) + diffs[2] * wide(tinted, at, 2)
                gap = pulls - behind
                out.append(weights[k : k + many] * gap)
                behind = behind + alphas[k : k + many] * gap
            d_h, d_l = split2(jnp.concatenate(out[::-1], axis=0))
            both = jnp.concatenate([d_h, d_l, weight_h[part, :], weight_l[part, :]], axis=1)
            sums[chunk] = jnp.transpose(dot(both, pixel_w[...]))
        sums = jnp.concatenate(sums, axis=1)
        moments = sums[:16]
        tint = sums[16 : 16 + tints] + sums[16 + tints : edge]
        s_0, s_u, s_v, s_uu, s_uv, s_vv = [LN2 * moments[m : m + 1] for m in range(6)]
        sum_x = far_x * s_0 + s_u
        sum_y = far_y * s_0 + s_v
        grads = [
            -(2.0 * con_a * sum_x + con_b * sum_y),
            -(con_b * sum_x + 2.0 * con_c * sum_y),
            far_x * (sum_x + s_u) + s_uu,
            far_x * sum_y + far_y * s_u + s_uv,
            far_y * (sum_y + s_v) + s_vv,
            s_0,
        ] + [
            jnp.sum(
                jnp.where(own, tint[many * ch : many * ch + many], 0.0), axis=0, keepdims=True
            )
            for ch in range(3)
        ]
        for feat in range(9):
            for part, piece in enumerate(split2(grads[feat])):
                spread[pl.ds((part * 9 + feat) * 16, 16), :] = jnp.where(
                    mask, piece.astype(F32), 0.0
                ).astype(BF16)
        total[...] += dot(spread[...], onehot[...], NT)

    for step in range(groups):
        group(step)
    grids = []
    for feat in range(9):
        grids.append(total[16 * feat + 144 : 16 * feat + 160] + total[16 * feat : 16 * feat + 16])
    grids.append(jnp.zeros((16, 256), F32))
    for pair in range(5):
        for j in range(4):
            lanes = slice(64 * j, 64 * j + 64)
            out_ref[pl.ds(80 * j + pair, 16, stride=5), :] = jnp.concatenate(
                [grids[2 * pair][:, lanes], grids[2 * pair + 1][:, lanes]], axis=1
            )


MANY = 16


def order_slots(slot_rows):
    tiles, slots = slot_rows.shape
    groups = tiles // MANY
    turned = slot_rows.reshape(groups, MANY, slots).transpose(0, 2, 1)
    return turned.reshape(groups, slots * MANY // 128, 128)


def render(recv, ordered, tile_ids, target):
    groups, rows = ordered.shape[0], ordered.shape[1] * 128
    tiles = groups * MANY
    depth = 32
    return pl.pallas_call(
        render_kernel,
        out_shape=(
            jax.ShapeDtypeStruct((3, tiles, 256), F32),
            jax.ShapeDtypeStruct((320, 128), F32),
        ),
        in_specs=[whole(pltpu.SMEM)] + [whole(pltpu.VMEM)] * 3,
        out_specs=(whole(pltpu.VMEM), whole(pltpu.VMEM)),
        scratch_shapes=[
            pltpu.VMEM((432, 256), BF16),
            pltpu.VMEM((depth, 256), BF16),
            pltpu.VMEM((depth, 384), BF16),
            pltpu.VMEM((288, 256), F32),
            pltpu.VMEM((groups, 256, rows), BF16),
            pltpu.VMEM((groups, depth, rows), F32),
            pltpu.VMEM((groups, rows, depth), BF16),
            pltpu.VMEM((groups, rows, 256), F32),
            pltpu.VMEM((groups, rows, 256), F32),
            pltpu.VMEM((groups, rows, 256), BF16),
            pltpu.VMEM((groups, rows, 256), BF16),
            pltpu.VMEM((groups, 1024, 128), BF16),
            pltpu.VMEM((groups, 288, rows), BF16),
            pltpu.VMEM((groups, rows, 384), F32),
        ],
        compiler_params=LIMIT,
        name="render",
    )(tile_ids, recv, ordered, target)


def camera_block(camera_ref, chosen_ref, block):
    lane = iota((8, 128), 1)
    sub = iota((8, 128), 0)
    which = jnp.zeros((8, 128), I32)
    for k in range(8):
        near = chosen_ref[0, block * 8 + k]
        far = chosen_ref[0, 32 + block * 8 + k]
        which = jnp.where(sub == k, jnp.where(lane < 64, near, far), which)
    values = [jnp.zeros((8, 128), F32) for _ in range(16)]
    for cam in range(16):
        here = which == cam
        values = [
            jnp.where(here, camera_ref[k, cam], value) for k, value in enumerate(values)
        ]
    return values


def row_index(send_ref, index):
    index[...] = jnp.concatenate([send_ref[:32, :], send_ref[32:, :]], axis=1)


def send_kernel(camera_ref, chosen_ref, send_ref, params_ref, out_ref, raw_ref, table, index, feats):
    row_index(send_ref, index)
    for hi in range(8):
        piece = params_ref[:, 512 * hi : 512 * hi + 512]
        piece = jnp.concatenate([piece, jnp.zeros((5, 512), F32)], axis=0)
        high, mid, low = split3(piece)
        table[144 * hi : 144 * hi + 64, :] = high
        table[144 * hi + 64 : 144 * hi + 128, :] = mid
        table[144 * hi + 128 : 144 * hi + 144, :] = low[:16]

    def pick(block):
        here = jnp.concatenate(
            [index[pl.ds(2 * block, 1), :], index[pl.ds(2 * block + 1, 1), :]], axis=1
        )
        onehot = jnp.where(iota((512, 256), 0) == (here & 511), 1.0, 0.0).astype(BF16)
        found = dot(table[...], onehot)
        bank = here >> 9
        value = jnp.zeros((64, 256), F32)
        for hi in range(8):
            high = found[144 * hi : 144 * hi + 64]
            mid = found[144 * hi + 64 : 144 * hi + 128]
            low = found[144 * hi + 128 : 144 * hi + 144]
            mid = jnp.concatenate([mid[:16] + low, mid[16:]], axis=0)
            value = jnp.where(bank == hi, high + mid, value)
        raw_ref[pl.ds(2 * block, 64, stride=32), :] = value[:, :128]
        raw_ref[pl.ds(2 * block + 1, 64, stride=32), :] = value[:, 128:]

    for block in range(16):
        pick(block)

    def shape(block, carry):
        camera = camera_block(camera_ref, chosen_ref, block)
        start = pl.multiple_of(block * 8, 8)
        raw = [raw_ref[pl.ds(32 * p + start, 8), :] for p in range(59)]
        for feat, value in enumerate(sent_features(raw, camera)):
            feats[pl.ds(32 * feat + start, 8), :] = value
        return carry

    lax.fori_loop(0, 4, shape, 0)
    for half in range(2):
        lanes = slice(64 * half, 64 * half + 64)
        for pair in range(5):
            left = feats[64 * pair : 64 * pair + 32, lanes]
            if pair < 4:
                right = feats[64 * pair + 32 : 64 * pair + 64, lanes]
            else:
                right = jnp.zeros((32, 64), F32)
            out_ref[pl.ds(160 * half + pair, 32, stride=5), :] = jnp.concatenate(
                [left, right], axis=1
            )


def one_hots(here, grads, first, block, spread, onehot):
    lanes = slice(128 * block, 128 * block + 128)
    onehot[:, lanes] = jnp.where(iota((512, 128), 0) == (here & 511), 1.0, 0.0).astype(BF16)
    bank = here >> 9
    high, mid = split2(grads[pl.ds(32 * first + block, 32, stride=32), :])
    both = jnp.concatenate([high, mid], axis=0)
    for hi in range(8):
        chosen = jnp.where(bank == hi, 1.0, 0.0).astype(BF16)
        spread[64 * hi : 64 * hi + 64, lanes] = both * chosen


def bank_rows(everything, hi):
    return everything[64 * hi : 64 * hi + 32] + everything[64 * hi + 32 : 64 * hi + 64]


def back_kernel(
    camera_ref, chosen_ref, send_ref, raw_ref, back_ref, low_ref, high_ref, rest_ref,
    index, feats, grads, spread, onehot,
):
    row_index(send_ref, index)
    for pair in range(5):
        near = back_ref[pl.ds(pair, 32, stride=5), :]
        far = back_ref[pl.ds(160 + pair, 32, stride=5), :]
        feats[64 * pair : 64 * pair + 32, :] = jnp.concatenate([near[:, :64], far[:, :64]], axis=1)
        feats[64 * pair + 32 : 64 * pair + 64, :] = jnp.concatenate(
            [near[:, 64:], far[:, 64:]], axis=1
        )

    def pull_back(block, carry):
        camera = camera_block(camera_ref, chosen_ref, block)
        start = pl.multiple_of(block * 8, 8)
        raw = [raw_ref[pl.ds(32 * p + start, 8), :] for p in range(59)]
        _, pull = jax.vjp(lambda rows: sent_features(rows, camera), raw)
        (found,) = pull([feats[pl.ds(32 * feat + start, 8), :] for feat in range(9)])
        for p in range(32):
            grads[pl.ds(32 * p + start, 8), :] = found[p]
        for ch in range(3):
            rest_ref[pl.ds(32 * ch + start, 8), :] = found[11 + ch] * (1.0 / sh_zero)
        for axis, value in enumerate(direction(raw, camera)):
            rest_ref[pl.ds(32 * (3 + axis) + start, 8), :] = value
        rest_ref[pl.ds(32 * 6 + start, 8), :] = index[pl.ds(start, 8), :].astype(F32)
        return carry

    lax.fori_loop(0, 4, pull_back, 0)
    everything = jnp.zeros((512, 512), F32)
    for part in range(4):
        for block in range(8 * part, 8 * part + 8):
            one_hots(index[pl.ds(block, 1), :], grads, 0, block, spread, onehot)
        lanes = slice(1024 * part, 1024 * part + 1024)
        everything = everything + dot(spread[:, lanes], onehot[:, lanes], NT)
    for hi in range(8):
        total = bank_rows(everything, hi)
        low_ref[:, 512 * hi : 512 * hi + 512] = total[:16]
        high_ref[:, 512 * hi : 512 * hi + 512] = total[16:]


def rest_kernel(*refs):
    *messages, out_ref, grads_all, spread_all, onehot_all = refs
    sums = messages[grads_all.shape[0] :]
    messages = messages[: grads_all.shape[0]]
    everything = jnp.zeros((512, 512), F32)
    for which, rest_ref in enumerate(messages):
        grads, spread, onehot = grads_all.at[which], spread_all.at[which], onehot_all.at[which]
        grads[27 * 32 :, :] = jnp.zeros((5 * 32, 128), F32)
        for start in range(0, 32, 8):
            rows = [rest_ref[32 * p + start : 32 * p + start + 8, :] for p in range(6)]
            basis = sh_basis(*rows[3:])
            for p in range(32, 59):
                k, ch = divmod(p - 11, 3)
                at = 32 * (p - 32) + start
                grads[at : at + 8, :] = basis[k] * rows[ch]
        for part in range(4):
            for block in range(8 * part, 8 * part + 8):
                here = rest_ref[pl.ds(6 * 32 + block, 1), :].astype(I32)
                one_hots(here, grads, 0, block, spread, onehot)
            lanes = slice(1024 * part, 1024 * part + 1024)
            everything = everything + dot(spread[:, lanes], onehot[:, lanes], NT)
    for hi in range(8):
        lanes = slice(512 * hi, 512 * hi + 512)
        total = bank_rows(everything, hi)[:27]
        for earlier in sums:
            total = total + earlier[:, lanes]
        out_ref[:, lanes] = total


def whole(space):
    return pl.BlockSpec(memory_space=space)


LIMIT = pltpu.CompilerParams(vmem_limit_bytes=56 * 1024 * 1024)


def send_rows(cameras, chosen, send, params):
    return pl.pallas_call(
        send_kernel,
        out_shape=(
            jax.ShapeDtypeStruct((320, 128), F32),
            jax.ShapeDtypeStruct((2048, 128), F32),
        ),
        in_specs=[whole(pltpu.SMEM), whole(pltpu.SMEM), whole(pltpu.VMEM), whole(pltpu.VMEM)],
        out_specs=(whole(pltpu.VMEM), whole(pltpu.VMEM)),
        scratch_shapes=[
            pltpu.VMEM((8 * 144, 512), BF16),
            pltpu.VMEM((32, 128), I32),
            pltpu.VMEM((9 * 32, 128), F32),
        ],
        compiler_params=LIMIT,
        name="send_rows",
    )(cameras, chosen, send, params)


def pull_rows(cameras, chosen, send, raw, back):
    return pl.pallas_call(
        back_kernel,
        out_shape=(
            jax.ShapeDtypeStruct((16, 4096), F32),
            jax.ShapeDtypeStruct((16, 4096), F32),
            jax.ShapeDtypeStruct((7 * 32, 128), F32),
        ),
        in_specs=[whole(pltpu.SMEM)] * 2 + [whole(pltpu.VMEM)] * 3,
        out_specs=(whole(pltpu.VMEM),) * 3,
        scratch_shapes=[
            pltpu.VMEM((32, 128), I32),
            pltpu.VMEM((10 * 32, 128), F32),
            pltpu.VMEM((32 * 32, 128), F32),
            pltpu.VMEM((512, 4096), BF16),
            pltpu.VMEM((512, 4096), BF16),
        ],
        compiler_params=LIMIT,
        name="pull_rows",
    )(cameras, chosen, send, raw, back)


def rest_rows(messages, sums=()):
    count = len(messages)
    return pl.pallas_call(
        rest_kernel,
        out_shape=jax.ShapeDtypeStruct((27, 4096), F32),
        in_specs=[whole(pltpu.VMEM)] * (count + len(sums)),
        out_specs=whole(pltpu.VMEM),
        scratch_shapes=[
            pltpu.VMEM((count, 32 * 32, 128), F32),
            pltpu.VMEM((count, 512, 4096), BF16),
            pltpu.VMEM((count, 512, 4096), BF16),
        ],
        compiler_params=LIMIT,
        cost_estimate=pl.CostEstimate(
            flops=count * (1 << 31), bytes_accessed=count * (1 << 22), transcendentals=0
        ),
        name="rest_rows",
    )(*messages, *sums)


def adam_update(params, adam_m, adam_v, gradient):
    rates = jnp.asarray(learn_rates, jnp.float32)[:, None]
    new_m = 0.9 * adam_m + 0.1 * gradient
    new_v = 0.999 * adam_v + 0.001 * gradient * gradient
    new_params = params - rates * (new_m / bias_first) / (jnp.sqrt(new_v / bias_second) + 1e-08)
    return (new_params, new_m, new_v)


def on_device(
    params, adam_m, adam_v, cameras, device_camera, send_index, slot_rows, tile_ids, target
):
    send = send_index[0, 0]
    outgoing, raw = send_rows(cameras, device_camera, send, params)
    incoming = lax.all_to_all(outgoing.reshape(64, 1, 640), "gs", 0, 0, tiled=True)
    colours, back = render(
        incoming.reshape(320, 128),
        order_slots(slot_rows[0, 0]),
        tile_ids[0],
        target[0, 0].transpose(1, 0, 2),
    )
    returned = lax.all_to_all(back.reshape(64, 1, 640), "gs", 0, 0, tiled=True)
    low, high, rest = pull_rows(cameras, device_camera, send, raw, returned.reshape(320, 128))
    near = [(i, i ^ 1) for i in range(4)]
    far = [(i, 3 - i) for i in range(4)]
    near_rest = lax.ppermute(rest, "img", near)
    far_rest = lax.ppermute(rest, "img", far)
    low, high = low + lax.ppermute(low, "img", near), high + lax.ppermute(high, "img", far)
    low, high, near_rest, far_rest = lax.optimization_barrier((low, high, near_rest, far_rest))
    across_rest = lax.ppermute(near_rest, "img", far)
    low, high = low + lax.ppermute(low, "img", far), high + lax.ppermute(high, "img", near)
    sums = [rest_rows([rest]), rest_rows([near_rest, far_rest])]
    tail = rest_rows([across_rest], sums)
    total = jnp.concatenate([low, high, tail], axis=0)
    new_params, new_m, new_v = adam_update(params, adam_m, adam_v, total)
    return (new_params, new_m, new_v, colours.transpose(1, 0, 2)[None, None])


def solution(mesh):
    return jax.shard_map(
        on_device,
        mesh=mesh,
        in_specs=(
            P(None, "gs"),
            P(None, "gs"),
            P(None, "gs"),
            P(),
            P("img", None),
            P("img", "gs", None, None),
            P("img", "gs", None, None),
            P("img", "gs", None),
            P("img", "gs", None, None, None),
        ),
        out_specs=(P(None, "gs"), P(None, "gs"), P(None, "gs"), P("img", "gs", None, None, None)),
        check_vma=False,
    )
```

```python
import jax
import jax.numpy as jnp
import numpy as np
from jax import lax
from jax.experimental import pallas as pl
from jax.experimental.pallas import tpu as pltpu
from jax.sharding import PartitionSpec as P

TILE = 16
IMG_TILES = 16


sh_zero = 0.28209479177387814
sh_one = 0.4886025119029199
sh_two = (
    1.0925484305920792,
    -1.0925484305920792,
    0.31539156525252005,
    -1.0925484305920792,
    0.5462742152960396,
)
sh_three = (
    -0.5900435899266435,
    2.890611442640554,
    -0.4570457994644658,
    0.3731763325901154,
    -0.4570457994644658,
    1.445305721320277,
    -0.5900435899266435,
)
learn_rates = np.array(
    [0.00016] * 3 + [0.005] * 3 + [0.001] * 4 + [0.05] + [0.0025] * 3 + [0.000125] * 45
)
LN2 = float(np.log(2.0))
LOG2_E = 1.0 / LN2
LOG_TOP = float(np.log2(0.99))
bias_first = 1.0 - 0.9**10
bias_second = 1.0 - 0.999**10


def sh_basis(dir_x, dir_y, dir_z):
    square_x = dir_x * dir_x
    square_y = dir_y * dir_y
    square_z = dir_z * dir_z
    return [
        sh_zero * jnp.ones_like(dir_x),
        -sh_one * dir_y,
        sh_one * dir_z,
        -sh_one * dir_x,
        sh_two[0] * dir_x * dir_y,
        sh_two[1] * dir_y * dir_z,
        sh_two[2] * (2.0 * square_z - square_x - square_y),
        sh_two[3] * dir_x * dir_z,
        sh_two[4] * (square_x - square_y),
        sh_three[0] * dir_y * (3.0 * square_x - square_y),
        sh_three[1] * dir_x * dir_y * dir_z,
        sh_three[2] * dir_y * (4.0 * square_z - square_x - square_y),
        sh_three[3] * dir_z * (2.0 * square_z - 3.0 * square_x - 3.0 * square_y),
        sh_three[4] * dir_x * (4.0 * square_z - square_x - square_y),
        sh_three[5] * dir_z * (square_x - square_y),
        sh_three[6] * dir_x * (square_x - 3.0 * square_y),
    ]


def direction(raw, camera):
    ray = [raw[first] - camera[12 + first] for first in range(3)]
    ray_scale = lax.rsqrt(ray[0] * ray[0] + ray[1] * ray[1] + ray[2] * ray[2])
    return [ray[0] * ray_scale, ray[1] * ray_scale, ray[2] * ray_scale]


def sent_features(raw, camera):
    world = [raw[0], raw[1], raw[2]]
    scales = [jnp.exp(raw[3]), jnp.exp(raw[4]), jnp.exp(raw[5])]
    quat_sq = jnp.maximum(
        raw[6] * raw[6] + raw[7] * raw[7] + raw[8] * raw[8] + raw[9] * raw[9], 0.25
    )
    inverse = lax.rsqrt(quat_sq)
    quat_w, quat_x, quat_y, quat_z = (
        raw[6] * inverse,
        raw[7] * inverse,
        raw[8] * inverse,
        raw[9] * inverse,
    )
    rotation = [
        [
            1.0 - 2.0 * (quat_y * quat_y + quat_z * quat_z),
            2.0 * (quat_x * quat_y - quat_w * quat_z),
            2.0 * (quat_x * quat_z + quat_w * quat_y),
        ],
        [
            2.0 * (quat_x * quat_y + quat_w * quat_z),
            1.0 - 2.0 * (quat_x * quat_x + quat_z * quat_z),
            2.0 * (quat_y * quat_z - quat_w * quat_x),
        ],
        [
            2.0 * (quat_x * quat_z - quat_w * quat_y),
            2.0 * (quat_y * quat_z + quat_w * quat_x),
            1.0 - 2.0 * (quat_x * quat_x + quat_y * quat_y),
        ],
    ]
    spread = [
        [rotation[first][second] * scales[second] for second in range(3)] for first in range(3)
    ]
    turn = [[camera[3 * first + second] for second in range(3)] for first in range(3)]
    viewed = [
        turn[first][0] * world[0]
        + turn[first][1] * world[1]
        + turn[first][2] * world[2]
        + camera[9 + first]
        for first in range(3)
    ]
    inv_depth = 1.0 / viewed[2]
    focal = camera[15]
    jacobian = [
        [focal * inv_depth, 0.0 * inv_depth, -focal * viewed[0] * inv_depth * inv_depth],
        [0.0 * inv_depth, focal * inv_depth, -focal * viewed[1] * inv_depth * inv_depth],
    ]
    screen = [
        [
            sum((jacobian[first][inner] * turn[inner][second] for inner in range(3)))
            for second in range(3)
        ]
        for first in range(2)
    ]
    mapped = [
        [
            sum((screen[first][inner] * spread[inner][second] for inner in range(3)))
            for second in range(3)
        ]
        for first in range(2)
    ]
    cov_xx = sum((mapped[0][inner] * mapped[0][inner] for inner in range(3))) + 0.3
    cov_xy = sum((mapped[0][inner] * mapped[1][inner] for inner in range(3)))
    cov_yy = sum((mapped[1][inner] * mapped[1][inner] for inner in range(3))) + 0.3
    determinant = cov_xx * cov_yy - cov_xy * cov_xy
    half_width = 0.5 * IMG_TILES * TILE
    basis = sh_basis(*direction(raw, camera))
    colours = [
        jnp.maximum(
            sum((basis[term] * raw[11 + 3 * term + channel] for term in range(16))) + 0.5, 0.0
        )
        for channel in range(3)
    ]
    inverse_det = 1.0 / determinant
    log_opacity = LOG_TOP - jnp.log(1.0 + jnp.exp(-raw[10])) * LOG2_E
    return [
        focal * viewed[0] * inv_depth + half_width,
        focal * viewed[1] * inv_depth + half_width,
        (-0.5 * LOG2_E) * cov_yy * inverse_det,
        LOG2_E * cov_xy * inverse_det,
        (-0.5 * LOG2_E) * cov_xx * inverse_det,
        log_opacity,
        colours[0],
        colours[1],
        colours[2],
    ]


F32, BF16, I32 = jnp.float32, jnp.bfloat16, jnp.int32
NN = (((1,), (0,)), ((), ()))
NT = (((1,), (1,)), ((), ()))


def dot(left, right, dims=NN):
    return lax.dot_general(left, right, dims, preferred_element_type=F32)


def split2(value):
    high = value.astype(BF16)
    return high, (value - high.astype(F32)).astype(BF16)


def split3(value):
    high = value.astype(BF16)
    rest = value - high.astype(F32)
    mid = rest.astype(BF16)
    return high, mid, (rest - mid.astype(F32)).astype(BF16)


def iota(shape, dim):
    return lax.broadcasted_iota(I32, shape, dim)


def wide(tinted, at, ch):
    value = tinted[at, 128 * ch : 128 * ch + 128]
    return jnp.concatenate([value, value], axis=1)


def render_kernel(
    tid_ref, recv_ref, slots_ref, target_ref, colour_ref, out_ref,
    table, onehot, coef, power_w, turned, alpha, weight, weight_h, weight_l, pixel_w,
    spread, total, tint_w, tinted,
):
    groups, rows = slots_ref.shape[0], slots_ref.shape[1] * 128
    many = target_ref.shape[1] // groups
    tints = 3 * many
    edge = 16 + 2 * tints
    chunks = rows // 256
    depth = coef.shape[0]
    for feat in range(9):
        side = slice(64 * (feat % 2), 64 * (feat % 2) + 64)
        block = jnp.concatenate(
            [recv_ref[pl.ds(80 * j + feat // 2, 16, stride=5), :][:, side] for j in range(4)],
            axis=1,
        )
        for part, piece in enumerate(split3(block)):
            table[pl.ds((part * 9 + feat) * 16, 16), :] = piece
    total[...] = jnp.zeros_like(total)
    coef[...] = jnp.zeros_like(coef)
    def pick(kind, u, v):
        out = jnp.where(kind == 0, 1.0, 0.0)
        out = jnp.where(kind == 1, u, out)
        out = jnp.where(kind == 2, v, out)
        out = jnp.where(kind == 3, u * u, out)
        out = jnp.where(kind == 4, u * v, out)
        return jnp.where(kind == 5, v * v, out)
    pix = iota((256, 128), 0)
    mono = pick(
        iota((256, 128), 1), (pix & 15).astype(F32) - 7.5, (pix >> 4).astype(F32) - 7.5
    ).astype(BF16)
    pixel_w[:256, :] = mono
    pixel_w[256:512, :] = mono
    row = iota((depth, 256), 0)
    pix = iota((depth, 256), 1)
    kind = jnp.where(row >= 12, row - 12, jnp.where(row >= 6, row - 6, row))
    power_w[...] = jnp.where(
        row < 18,
        pick(kind, (pix & 15).astype(F32) - 7.5, (pix >> 4).astype(F32) - 7.5),
        0.0,
    ).astype(BF16)

    row = iota((depth, 384), 0)
    first_row = 18 + 3 * (iota((depth, 384), 1) >> 7)
    tint_w[...] = jnp.where((row >= first_row) & (row < first_row + 3), 1.0, 0.0).astype(BF16)

    lane_tile = iota((1, rows), 1) & (many - 1)
    own = iota((many, rows), 0) == lane_tile
    hi_row = iota((16, rows), 0)

    def group(step, carry):
        index = jnp.concatenate(
            [slots_ref[step, pl.ds(block, 1), :] for block in range(rows // 128)], axis=1
        )
        live = index >= 0
        low = ((index >> 10) << 6) | (index & 63)
        high = jnp.where(live, (index >> 6) & 15, -1)
        onehot[...] = jnp.where(iota((256, rows), 0) == low, 1.0, 0.0).astype(BF16)
        mask = hi_row == high
        raw = dot(table[...], onehot[...])
        feats = []
        for feat in range(9):
            part = (
                raw[288 + 16 * feat : 304 + 16 * feat] + raw[144 + 16 * feat : 160 + 16 * feat]
            ) + raw[16 * feat : 16 * feat + 16]
            feats.append(jnp.sum(jnp.where(mask, part, 0.0), axis=0, keepdims=True))
        mean_x, mean_y, con_a, con_b, con_c, log_op = feats[:6]
        centre_x = jnp.zeros((1, rows), F32)
        centre_y = jnp.zeros((1, rows), F32)
        for t in range(many):
            tid = tid_ref[0, step * many + t]
            centre_x = jnp.where(lane_tile == t, ((tid & 15) * 16 + 8).astype(F32), centre_x)
            centre_y = jnp.where(lane_tile == t, ((tid >> 4) * 16 + 8).astype(F32), centre_y)
        far_x = centre_x - mean_x
        far_y = centre_y - mean_y
        ax = con_a * far_x
        bx = con_b * far_x
        by = con_b * far_y
        cy = con_c * far_y
        constant = far_x * (ax + by) + far_y * cy + log_op
        constant = jnp.where(live, constant, -1e30)
        for m, value in enumerate(
            (constant, 2.0 * ax + by, bx + 2.0 * cy, con_a, con_b, con_c)
        ):
            for part, piece in enumerate(split3(value)):
                coef[pl.ds(part * 6 + m, 1), :] = piece.astype(F32)
        for ch in range(3):
            for part, piece in enumerate(split3(feats[6 + ch])):
                coef[pl.ds(18 + 3 * ch + part, 1), :] = piece.astype(F32)
        turned[...] = jnp.transpose(coef[...]).astype(BF16)

        passed = jnp.ones((many, 256), F32)
        shown = [jnp.zeros((many, 256), F32)] * 3
        for chunk in range(chunks):
            part = slice(256 * chunk, 256 * chunk + 256)
            alphas = jnp.exp2(dot(turned[part, :], power_w[...]))
            tinted[part, :] = dot(turned[part, :], tint_w[...])
            alpha[part, :] = alphas
            out = []
            for k in range(0, 256, many):
                w = passed * alphas[k : k + many]
                passed = passed - w
                at = slice(256 * chunk + k, 256 * chunk + k + many)
                shown = [value + w * wide(tinted, at, ch) for ch, value in enumerate(shown)]
                out.append(w)
            out = jnp.concatenate(out, axis=0)
            weight[part, :] = out
            w_h, w_l = split2(out)
            weight_h[part, :] = w_h
            weight_l[part, :] = w_l
        diffs = []
        for ch in range(3):
            where = pl.ds(pl.multiple_of(step * many, many), many)
            colour_ref[ch, where, :] = shown[ch]
            diffs.append(shown[ch] - target_ref[ch, where, :])
        d_high = [value.astype(BF16).astype(F32) for value in diffs]
        d_mid = [value - high for value, high in zip(diffs, d_high)]
        front = jnp.zeros((16, 256), F32)
        back = jnp.zeros((128 - edge, 256), F32)
        pixel_w[512:768, :] = jnp.transpose(
            jnp.concatenate([front] + d_high + d_mid + [back], axis=0)
        ).astype(BF16)
        pixel_w[768:, :] = jnp.transpose(
            jnp.concatenate([front] + d_high + [jnp.zeros((112 - tints, 256), F32)], axis=0)
        ).astype(BF16)

        behind = jnp.zeros((many, 256), F32)
        sums = [None] * chunks
        for chunk in range(chunks - 1, -1, -1):
            part = slice(256 * chunk, 256 * chunk + 256)
            alphas = alpha[part, :]
            weights = weight[part, :]
            out = []
            for k in range(256 - many, -1, -many):
                at = slice(256 * chunk + k, 256 * chunk + k + many)
                pulls = (
                    diffs[0] * wide(tinted, at, 0) + diffs[1] * wide(tinted, at, 1)
                ) + diffs[2] * wide(tinted, at, 2)
                gap = pulls - behind
                out.append(weights[k : k + many] * gap)
                behind = behind + alphas[k : k + many] * gap
            d_h, d_l = split2(jnp.concatenate(out[::-1], axis=0))
            both = jnp.concatenate([d_h, d_l, weight_h[part, :], weight_l[part, :]], axis=1)
            sums[chunk] = jnp.transpose(dot(both, pixel_w[...]))
        sums = jnp.concatenate(sums, axis=1)
        moments = sums[:16]
        tint = sums[16 : 16 + tints] + sums[16 + tints : edge]
        s_0, s_u, s_v, s_uu, s_uv, s_vv = [LN2 * moments[m : m + 1] for m in range(6)]
        sum_x = far_x * s_0 + s_u
        sum_y = far_y * s_0 + s_v
        grads = [
            -(2.0 * con_a * sum_x + con_b * sum_y),
            -(con_b * sum_x + 2.0 * con_c * sum_y),
            far_x * (sum_x + s_u) + s_uu,
            far_x * sum_y + far_y * s_u + s_uv,
            far_y * (sum_y + s_v) + s_vv,
            s_0,
        ] + [
            jnp.sum(
                jnp.where(own, tint[many * ch : many * ch + many], 0.0), axis=0, keepdims=True
            )
            for ch in range(3)
        ]
        for feat in range(9):
            for part, piece in enumerate(split2(grads[feat])):
                spread[pl.ds((part * 9 + feat) * 16, 16), :] = jnp.where(
                    mask, piece.astype(F32), 0.0
                ).astype(BF16)
        total[...] += dot(spread[...], onehot[...], NT)
        return carry

    lax.fori_loop(0, groups, group, 0)
    grids = []
    for feat in range(9):
        grids.append(total[16 * feat + 144 : 16 * feat + 160] + total[16 * feat : 16 * feat + 16])
    grids.append(jnp.zeros((16, 256), F32))
    for pair in range(5):
        for j in range(4):
            lanes = slice(64 * j, 64 * j + 64)
            out_ref[pl.ds(80 * j + pair, 16, stride=5), :] = jnp.concatenate(
                [grids[2 * pair][:, lanes], grids[2 * pair + 1][:, lanes]], axis=1
            )


MANY = 16


def order_slots(slot_rows):
    tiles, slots = slot_rows.shape
    groups = tiles // MANY
    turned = slot_rows.reshape(groups, MANY, slots).transpose(0, 2, 1)
    return turned.reshape(groups, slots * MANY // 128, 128)


def render(recv, ordered, tile_ids, target):
    groups, rows = ordered.shape[0], ordered.shape[1] * 128
    tiles = groups * MANY
    depth = 32
    return pl.pallas_call(
        render_kernel,
        out_shape=(
            jax.ShapeDtypeStruct((3, tiles, 256), F32),
            jax.ShapeDtypeStruct((320, 128), F32),
        ),
        in_specs=[whole(pltpu.SMEM)] + [whole(pltpu.VMEM)] * 3,
        out_specs=(whole(pltpu.VMEM), whole(pltpu.VMEM)),
        scratch_shapes=[
            pltpu.VMEM((432, 256), BF16),
            pltpu.VMEM((256, rows), BF16),
            pltpu.VMEM((depth, rows), F32),
            pltpu.VMEM((depth, 256), BF16),
            pltpu.VMEM((rows, depth), BF16),
            pltpu.VMEM((rows, 256), F32),
            pltpu.VMEM((rows, 256), F32),
            pltpu.VMEM((rows, 256), BF16),
            pltpu.VMEM((rows, 256), BF16),
            pltpu.VMEM((1024, 128), BF16),
            pltpu.VMEM((288, rows), BF16),
            pltpu.VMEM((288, 256), F32),
            pltpu.VMEM((depth, 384), BF16),
            pltpu.VMEM((rows, 384), F32),
        ],
        compiler_params=LIMIT,
        name="render",
    )(tile_ids, recv, ordered, target)


def camera_block(camera_ref, chosen_ref, block):
    lane = iota((8, 128), 1)
    sub = iota((8, 128), 0)
    which = jnp.zeros((8, 128), I32)
    for k in range(8):
        near = chosen_ref[0, block * 8 + k]
        far = chosen_ref[0, 32 + block * 8 + k]
        which = jnp.where(sub == k, jnp.where(lane < 64, near, far), which)
    values = [jnp.zeros((8, 128), F32) for _ in range(16)]
    for cam in range(16):
        here = which == cam
        values = [
            jnp.where(here, camera_ref[k, cam], value) for k, value in enumerate(values)
        ]
    return values


def row_index(send_ref, index):
    index[...] = jnp.concatenate([send_ref[:32, :], send_ref[32:, :]], axis=1)


def send_kernel(camera_ref, chosen_ref, send_ref, params_ref, out_ref, raw_ref, table, index, feats):
    row_index(send_ref, index)
    for hi in range(8):
        piece = params_ref[:, 512 * hi : 512 * hi + 512]
        piece = jnp.concatenate([piece, jnp.zeros((5, 512), F32)], axis=0)
        high, mid, low = split3(piece)
        table[144 * hi : 144 * hi + 64, :] = high
        table[144 * hi + 64 : 144 * hi + 128, :] = mid
        table[144 * hi + 128 : 144 * hi + 144, :] = low[:16]

    def pick(block):
        here = jnp.concatenate(
            [index[pl.ds(2 * block, 1), :], index[pl.ds(2 * block + 1, 1), :]], axis=1
        )
        onehot = jnp.where(iota((512, 256), 0) == (here & 511), 1.0, 0.0).astype(BF16)
        found = dot(table[...], onehot)
        bank = here >> 9
        value = jnp.zeros((64, 256), F32)
        for hi in range(8):
            high = found[144 * hi : 144 * hi + 64]
            mid = found[144 * hi + 64 : 144 * hi + 128]
            low = found[144 * hi + 128 : 144 * hi + 144]
            mid = jnp.concatenate([mid[:16] + low, mid[16:]], axis=0)
            value = jnp.where(bank == hi, high + mid, value)
        raw_ref[pl.ds(2 * block, 64, stride=32), :] = value[:, :128]
        raw_ref[pl.ds(2 * block + 1, 64, stride=32), :] = value[:, 128:]

    for block in range(16):
        pick(block)

    def shape(block, carry):
        camera = camera_block(camera_ref, chosen_ref, block)
        start = pl.multiple_of(block * 8, 8)
        raw = [raw_ref[pl.ds(32 * p + start, 8), :] for p in range(59)]
        for feat, value in enumerate(sent_features(raw, camera)):
            feats[pl.ds(32 * feat + start, 8), :] = value
        return carry

    lax.fori_loop(0, 4, shape, 0)
    for half in range(2):
        lanes = slice(64 * half, 64 * half + 64)
        for pair in range(5):
            left = feats[64 * pair : 64 * pair + 32, lanes]
            if pair < 4:
                right = feats[64 * pair + 32 : 64 * pair + 64, lanes]
            else:
                right = jnp.zeros((32, 64), F32)
            out_ref[pl.ds(160 * half + pair, 32, stride=5), :] = jnp.concatenate(
                [left, right], axis=1
            )


def one_hots(here, grads, first, block, spread, onehot):
    lanes = slice(128 * block, 128 * block + 128)
    onehot[:, lanes] = jnp.where(iota((512, 128), 0) == (here & 511), 1.0, 0.0).astype(BF16)
    bank = here >> 9
    high, mid = split2(grads[pl.ds(32 * first + block, 32, stride=32), :])
    both = jnp.concatenate([high, mid], axis=0)
    for hi in range(8):
        chosen = jnp.where(bank == hi, 1.0, 0.0).astype(BF16)
        spread[64 * hi : 64 * hi + 64, lanes] = both * chosen


def bank_rows(everything, hi):
    return everything[64 * hi : 64 * hi + 32] + everything[64 * hi + 32 : 64 * hi + 64]


def back_kernel(
    camera_ref, chosen_ref, send_ref, raw_ref, back_ref, low_ref, high_ref, rest_ref,
    index, feats, grads, spread, onehot,
):
    row_index(send_ref, index)
    for pair in range(5):
        near = back_ref[pl.ds(pair, 32, stride=5), :]
        far = back_ref[pl.ds(160 + pair, 32, stride=5), :]
        feats[64 * pair : 64 * pair + 32, :] = jnp.concatenate([near[:, :64], far[:, :64]], axis=1)
        feats[64 * pair + 32 : 64 * pair + 64, :] = jnp.concatenate(
            [near[:, 64:], far[:, 64:]], axis=1
        )

    def pull_back(block, carry):
        camera = camera_block(camera_ref, chosen_ref, block)
        start = pl.multiple_of(block * 8, 8)
        raw = [raw_ref[pl.ds(32 * p + start, 8), :] for p in range(59)]
        _, pull = jax.vjp(lambda rows: sent_features(rows, camera), raw)
        (found,) = pull([feats[pl.ds(32 * feat + start, 8), :] for feat in range(9)])
        for p in range(32):
            grads[pl.ds(32 * p + start, 8), :] = found[p]
        for ch in range(3):
            rest_ref[pl.ds(32 * ch + start, 8), :] = found[11 + ch] * (1.0 / sh_zero)
        for axis, value in enumerate(direction(raw, camera)):
            rest_ref[pl.ds(32 * (3 + axis) + start, 8), :] = value
        rest_ref[pl.ds(32 * 6 + start, 8), :] = index[pl.ds(start, 8), :].astype(F32)
        return carry

    lax.fori_loop(0, 4, pull_back, 0)
    everything = jnp.zeros((512, 512), F32)
    for part in range(4):
        for block in range(8 * part, 8 * part + 8):
            one_hots(index[pl.ds(block, 1), :], grads, 0, block, spread, onehot)
        lanes = slice(1024 * part, 1024 * part + 1024)
        everything = everything + dot(spread[:, lanes], onehot[:, lanes], NT)
    for hi in range(8):
        total = bank_rows(everything, hi)
        low_ref[:, 512 * hi : 512 * hi + 512] = total[:16]
        high_ref[:, 512 * hi : 512 * hi + 512] = total[16:]


def rest_kernel(*refs):
    *messages, out_ref, grads_all, spread_all, onehot_all = refs
    sums = messages[grads_all.shape[0] :]
    messages = messages[: grads_all.shape[0]]
    everything = jnp.zeros((512, 512), F32)
    for which, rest_ref in enumerate(messages):
        grads, spread, onehot = grads_all.at[which], spread_all.at[which], onehot_all.at[which]
        grads[27 * 32 :, :] = jnp.zeros((5 * 32, 128), F32)
        for start in range(0, 32, 8):
            rows = [rest_ref[32 * p + start : 32 * p + start + 8, :] for p in range(6)]
            basis = sh_basis(*rows[3:])
            for p in range(32, 59):
                k, ch = divmod(p - 11, 3)
                at = 32 * (p - 32) + start
                grads[at : at + 8, :] = basis[k] * rows[ch]
        for part in range(4):
            for block in range(8 * part, 8 * part + 8):
                here = rest_ref[pl.ds(6 * 32 + block, 1), :].astype(I32)
                one_hots(here, grads, 0, block, spread, onehot)
            lanes = slice(1024 * part, 1024 * part + 1024)
            everything = everything + dot(spread[:, lanes], onehot[:, lanes], NT)
    for hi in range(8):
        lanes = slice(512 * hi, 512 * hi + 512)
        total = bank_rows(everything, hi)[:27]
        for earlier in sums:
            total = total + earlier[:, lanes]
        out_ref[:, lanes] = total


def whole(space):
    return pl.BlockSpec(memory_space=space)


LIMIT = pltpu.CompilerParams(vmem_limit_bytes=56 * 1024 * 1024)


def send_rows(cameras, chosen, send, params):
    return pl.pallas_call(
        send_kernel,
        out_shape=(
            jax.ShapeDtypeStruct((320, 128), F32),
            jax.ShapeDtypeStruct((2048, 128), F32),
        ),
        in_specs=[whole(pltpu.SMEM), whole(pltpu.SMEM), whole(pltpu.VMEM), whole(pltpu.VMEM)],
        out_specs=(whole(pltpu.VMEM), whole(pltpu.VMEM)),
        scratch_shapes=[
            pltpu.VMEM((8 * 144, 512), BF16),
            pltpu.VMEM((32, 128), I32),
            pltpu.VMEM((9 * 32, 128), F32),
        ],
        compiler_params=LIMIT,
        name="send_rows",
    )(cameras, chosen, send, params)


def pull_rows(cameras, chosen, send, raw, back):
    return pl.pallas_call(
        back_kernel,
        out_shape=(
            jax.ShapeDtypeStruct((16, 4096), F32),
            jax.ShapeDtypeStruct((16, 4096), F32),
            jax.ShapeDtypeStruct((7 * 32, 128), F32),
        ),
        in_specs=[whole(pltpu.SMEM)] * 2 + [whole(pltpu.VMEM)] * 3,
        out_specs=(whole(pltpu.VMEM),) * 3,
        scratch_shapes=[
            pltpu.VMEM((32, 128), I32),
            pltpu.VMEM((10 * 32, 128), F32),
            pltpu.VMEM((32 * 32, 128), F32),
            pltpu.VMEM((512, 4096), BF16),
            pltpu.VMEM((512, 4096), BF16),
        ],
        compiler_params=LIMIT,
        name="pull_rows",
    )(cameras, chosen, send, raw, back)


def rest_rows(messages, sums=()):
    count = len(messages)
    return pl.pallas_call(
        rest_kernel,
        out_shape=jax.ShapeDtypeStruct((27, 4096), F32),
        in_specs=[whole(pltpu.VMEM)] * (count + len(sums)),
        out_specs=whole(pltpu.VMEM),
        scratch_shapes=[
            pltpu.VMEM((count, 32 * 32, 128), F32),
            pltpu.VMEM((count, 512, 4096), BF16),
            pltpu.VMEM((count, 512, 4096), BF16),
        ],
        compiler_params=LIMIT,
        cost_estimate=pl.CostEstimate(
            flops=count * (1 << 31), bytes_accessed=count * (1 << 22), transcendentals=0
        ),
        name="rest_rows",
    )(*messages, *sums)


def adam_update(params, adam_m, adam_v, gradient):
    rates = jnp.asarray(learn_rates, jnp.float32)[:, None]
    new_m = 0.9 * adam_m + 0.1 * gradient
    new_v = 0.999 * adam_v + 0.001 * gradient * gradient
    new_params = params - rates * (new_m / bias_first) / (jnp.sqrt(new_v / bias_second) + 1e-08)
    return (new_params, new_m, new_v)


def on_device(
    params, adam_m, adam_v, cameras, device_camera, send_index, slot_rows, tile_ids, target
):
    send = send_index[0, 0]
    outgoing, raw = send_rows(cameras, device_camera, send, params)
    incoming = lax.all_to_all(outgoing.reshape(64, 1, 640), "gs", 0, 0, tiled=True)
    colours, back = render(
        incoming.reshape(320, 128),
        order_slots(slot_rows[0, 0]),
        tile_ids[0],
        target[0, 0].transpose(1, 0, 2),
    )
    returned = lax.all_to_all(back.reshape(64, 1, 640), "gs", 0, 0, tiled=True)
    low, high, rest = pull_rows(cameras, device_camera, send, raw, returned.reshape(320, 128))
    near = [(i, i ^ 1) for i in range(4)]
    far = [(i, 3 - i) for i in range(4)]
    near_rest = lax.ppermute(rest, "img", near)
    far_rest = lax.ppermute(rest, "img", far)
    low, high = low + lax.ppermute(low, "img", near), high + lax.ppermute(high, "img", far)
    rest, near_rest = lax.optimization_barrier((rest, near_rest))
    across_rest = lax.ppermute(near_rest, "img", far)
    own = rest_rows([rest])
    low, high, far_rest, across_rest = lax.optimization_barrier(
        (low, high, far_rest, across_rest)
    )
    low, high = low + lax.ppermute(low, "img", far), high + lax.ppermute(high, "img", near)
    tail = rest_rows([near_rest, far_rest, across_rest], [own])
    total = jnp.concatenate([low, high, tail], axis=0)
    new_params, new_m, new_v = adam_update(params, adam_m, adam_v, total)
    return (new_params, new_m, new_v, colours.transpose(1, 0, 2)[None, None])


def solution(mesh):
    return jax.shard_map(
        on_device,
        mesh=mesh,
        in_specs=(
            P(None, "gs"),
            P(None, "gs"),
            P(None, "gs"),
            P(),
            P("img", None),
            P("img", "gs", None, None),
            P("img", "gs", None, None),
            P("img", "gs", None),
            P("img", "gs", None, None, None),
        ),
        out_specs=(P(None, "gs"), P(None, "gs"), P(None, "gs"), P("img", "gs", None, None, None)),
        check_vma=False,
    )
```
